256 devices in a mesh: row: 8 (over z), col: 32 (over x, y, core).
Axes of the slice: x: 4, y: 4, z: 8, core: 2. Of those that a mesh axis runs over, the one named last changes fastest.
Arguments:
- embeddings: bfloat16 [49152, 256], P(('row', 'col')), may hold values from -256 to 256
- start_vectors: float32 [49152, 64], P(('row', 'col')), may hold values from -6 to 6
Outputs:
- spectral: float32 [49152, 64], P(('row', 'col'))
The draws below stay inside these ranges and needn't reach their ends.
All inputs are finite; a program needn't handle non-finite values.
Results may differ from the reference program's by a relative error of at most 0.0068.
Values may be sent and summed in bfloat16 or wider, within the bound.
No kernel may reach another device: no remote copies, remote signals or barrier semaphores. Data moves between devices by JAX's collectives and lax.ppermute only.
A program may use at most 64 MiB of HBM per device.

```python
import math
import jax
import jax.numpy as jnp
from jax import lax

E = 256
K = 64
ITERS = 2
DOCS = 49152


def draw_embeddings(key, part):
    key = jax.random.fold_in(key, 11)
    key_noise, key_shared, key_weight, key_scale = jax.random.split(key, 4)
    noise = jnp.clip(jax.random.normal(key_noise, (DOCS, E), jnp.float32), -5.0, 5.0)
    widest = math.log(10.0)
    shared = jnp.clip(jax.random.normal(key_shared, (E,), jnp.float32), -4.0, 4.0)
    position = jnp.arange(DOCS, dtype=jnp.float32) / DOCS
    factor = jax.random.uniform(key_weight, (DOCS, 1), jnp.float32, 0.5, 1.5)
    mixing = 1.5 * position[:, None] * factor
    row_scale = jnp.exp(jax.random.uniform(key_scale, (DOCS, 1), jnp.float32, 0.0, widest))
    return ((noise + mixing * shared[None, :]) * row_scale).astype(jnp.bfloat16)


def shard_levels(own_key, shape, shards, smallest, largest):
    gain, own = 1.0, jax.random.fold_in(own_key, 6)
    for dim, shards_of in shards:
        draws = jnp.exp(jax.random.uniform(jax.random.fold_in(own, dim), (shards_of,), jnp.float32, smallest / len(shards), largest / len(shards)))
        gain = gain * jnp.repeat(draws, shape[dim] // shards_of).reshape([-1 if axis == dim else 1 for axis in range(len(shape))])
    return gain


def scatter_about(key, dims, spread, reach, pieces=(), kind=jnp.bfloat16):
    gain = shard_levels(key, dims, pieces, -0.22, 0.18) if pieces else 1.0
    drawn = jax.random.normal(key, dims, jnp.float32) * spread * gain
    return jnp.minimum(jnp.maximum(drawn, -reach), reach).astype(kind)


def setup_inputs(seed: int = 0) -> dict:
    key_of = jax.random.split(jax.random.key(seed), 3)
    embeddings = draw_embeddings(jax.random.fold_in(key_of[2], 71), 0)
    start_vectors = scatter_about(key_of[1], (DOCS, K), 1.0, 6.0, ((0, 256),), jnp.float32)
    return {"embeddings": embeddings, "start_vectors": start_vectors}


sharpness = 16.0
threshold = 0.3

def reference(embeddings, start_vectors):
    widened = embeddings.astype(jnp.float32)
    unit_rows = (widened * lax.rsqrt(lax.optimization_barrier(jnp.sum(widened * widened, axis=1, keepdims=True)) + 1e-06)).astype(jnp.bfloat16)
    rows_block = math.gcd(DOCS, 1024)
    doc_blocks = unit_rows.reshape(DOCS // rows_block, rows_block, E)

    def adjacency_rows(doc_block):
        scores = lax.dot_general(doc_block.astype(jnp.float32), unit_rows.astype(jnp.float32), (((1,), (1,)), ((), ())), preferred_element_type=jnp.float32)
        return jax.nn.sigmoid(sharpness * (scores - threshold)).astype(jnp.bfloat16)
    degree = lax.map(lambda doc_block: lax.optimization_barrier(jnp.sum(adjacency_rows(doc_block), axis=1, dtype=jnp.float32)), doc_blocks).reshape(DOCS)
    inv_root = lax.rsqrt(degree)
    root_degree = jnp.sqrt(degree)
    degree_total = jnp.sum(degree)
    vectors = start_vectors
    for iteration in range(ITERS):
        weighted = (inv_root[:, None] * vectors).astype(jnp.bfloat16)
        partial_sums = lax.map(lambda doc_block: jnp.dot(adjacency_rows(doc_block).astype(jnp.float32), weighted.astype(jnp.float32), preferred_element_type=jnp.float32), doc_blocks).reshape(DOCS, K)
        correlation = lax.optimization_barrier(jnp.sum(root_degree[:, None] * vectors, axis=0))
        vectors = inv_root[:, None] * partial_sums - root_degree[:, None] * (correlation / degree_total)[None, :]
    gram_matrix = jnp.dot(vectors.T, vectors, precision=lax.Precision.HIGHEST)
    cholesky_factor = jnp.linalg.cholesky(gram_matrix)
    solved = lax.linalg.triangular_solve(cholesky_factor, vectors.T, left_side=True, lower=True)
    return solved.T * math.sqrt(DOCS)
```

```python
import math

import jax
import jax.numpy as jnp
from jax import lax
from jax.sharding import Mesh
from jax.sharding import PartitionSpec as P

sharpness = 16.0
threshold = 0.3

AXES = ("z", "x", "y", "core")
PLANE = ("x", "y")
SIZES = {"z": 8, "x": 4, "y": 4, "core": 2}


def spread(value, axes):
    peers = math.prod(SIZES[a] for a in axes)
    return lax.all_to_all(
        jnp.broadcast_to(value[None], (peers, *value.shape)), axes, 0, 0, tiled=True
    )


def swap_core(value):
    return lax.ppermute(value, "core", [(0, 1), (1, 0)])


def rounded(value):
    return lax.reduce_precision(value, 8, 7)


def halves(value):
    hi = rounded(value)
    mid = rounded(value - hi)
    lo = value - hi - mid
    return tuple(part.astype(jnp.bfloat16) for part in (hi, mid, lo))


def local(embeddings, start_vectors):
    docs, width = embeddings.shape
    kept = start_vectors.shape[1]
    all_docs = docs * lax.axis_size(AXES)
    columns = docs * SIZES["z"]
    widened = embeddings.astype(jnp.float32)
    unit_rows = (
        widened * lax.rsqrt(jnp.sum(widened * widened, axis=1, keepdims=True) + 1e-06)
    ).astype(jnp.bfloat16)

    hi, mid, lo = halves(start_vectors)
    packed = jnp.concatenate([unit_rows, hi, mid], axis=1)
    column_set = spread(packed, ("z",)).reshape(columns, width + 2 * kept)
    column_units = column_set[:, :width]
    start = column_set[:, width : width + kept].astype(jnp.float32) + column_set[
        :, width + kept :
    ].astype(jnp.float32)
    own_side = spread(unit_rows, PLANE).reshape(-1, width)
    other_side = swap_core(own_side)

    def tile(rows):
        scores = lax.dot_general(
            rows, column_units, (((1,), (1,)), ((), ())), preferred_element_type=jnp.float32
        )
        return jax.nn.sigmoid(sharpness * (scores - threshold)).astype(jnp.bfloat16)

    tile_own = tile(own_side)
    tile_other = tile(other_side)
    sums = jnp.sum(tile_own, axis=0, dtype=jnp.float32) + jnp.sum(
        tile_other, axis=0, dtype=jnp.float32
    )
    degree = jnp.sum(spread(sums.reshape(columns // 128, 128), ("z",)).reshape(-1, columns), axis=0)
    inv_root = lax.rsqrt(degree)[:, None]
    root_degree = jnp.sqrt(degree)[:, None]

    first = lax.axis_index("z") * docs
    own_inv = lax.dynamic_slice_in_dim(inv_root, first, docs, 0)
    own_root = lax.dynamic_slice_in_dim(root_degree, first, docs, 0)

    def product(weighted, terms, kind):
        mine = jnp.dot(tile_other, weighted, preferred_element_type=jnp.float32)
        theirs = swap_core(mine)
        total = jnp.dot(tile_own, weighted, preferred_element_type=jnp.float32) + theirs
        sent = total.reshape(16, docs // 2, 2 * kept)
        if kind == jnp.bfloat16:
            extra = jnp.concatenate([*halves(terms)] * 2, axis=0)
        else:
            extra = terms
        extra = jnp.pad(extra, ((0, 16 - extra.shape[0]), (0, 0)))
        sent = jnp.concatenate(
            [sent.astype(kind), jnp.broadcast_to(extra[None], (16, *extra.shape))], axis=1
        )
        got = lax.all_to_all(sent, PLANE, 0, 0, tiled=True)
        sums = jnp.sum(got[:, : docs // 2].astype(jnp.float32), axis=0)
        rest = jnp.sum(got[:, docs // 2 :].astype(jnp.float32), axis=0)
        if kind == jnp.bfloat16:
            rest = rest[0:2] + rest[2:4] + rest[4:6]
        else:
            rest = rest[0:2]
        return sums.reshape(docs, kept), rest

    weighted = rounded(inv_root * start)
    total = jnp.full((kept,), 1.0) * jnp.sum(degree)
    terms = jnp.concatenate([jnp.sum(root_degree * start, axis=0), total]).reshape(1, -1)
    terms = jnp.concatenate([terms, jnp.zeros_like(terms)], axis=0)

    partial_sums, rest = product(weighted.astype(jnp.bfloat16), terms + swap_core(terms), jnp.bfloat16)
    correlation, degree_total = rest[0, :kept], rest[0, kept:]
    vectors = own_inv * partial_sums - own_root * (correlation / degree_total)[None, :]
    corr = jnp.sum(own_root * vectors, axis=0).reshape(1, kept)
    sent = jnp.concatenate(
        [rounded(own_inv * vectors).astype(jnp.bfloat16), *halves(corr), jnp.zeros((13, kept), jnp.bfloat16)], axis=0
    )
    got = spread(sent, ("z",)).reshape(-1, docs + 16, kept)
    corr = jnp.sum(got[:, docs : docs + 3].astype(jnp.float32), axis=(0, 1))
    corr = jnp.concatenate([corr, corr]).reshape(1, -1)
    corr = jnp.concatenate([corr, corr], axis=0)
    partial_sums, rest = product(
        got[:, :docs].reshape(columns, kept), corr + swap_core(corr), jnp.float32
    )
    vectors = own_inv * partial_sums - own_root * (rest[0, :kept] / degree_total)[None, :]

    gram = jnp.dot(vectors.T, vectors, precision=lax.Precision.HIGHEST)
    gram = jnp.concatenate([gram[: kept // 2], gram[kept // 2 :]], axis=1)
    gram = jnp.sum(spread(gram, ("z", "core")).reshape(16, kept // 2, 2 * kept), axis=0)
    gram = jnp.sum(spread(gram, PLANE).reshape(16, kept // 2, 2 * kept), axis=0)
    gram = jnp.concatenate([gram[:, :kept], gram[:, kept:]], axis=0)
    cholesky_factor = jnp.linalg.cholesky(gram)
    solved = lax.linalg.triangular_solve(cholesky_factor, vectors.T, left_side=True, lower=True)
    return solved.T * math.sqrt(all_docs)


def solution(mesh):
    fine = Mesh(mesh.devices.reshape(*SIZES.values()), AXES)
    return jax.shard_map(
        local,
        mesh=fine,
        in_specs=(P(AXES, None), P(AXES, None)),
        out_specs=P(AXES, None),
        check_vma=False,
    )
```

```python
import functools
import math

import jax
import jax.numpy as jnp
from jax import lax
from jax.experimental import pallas as pl
from jax.experimental.pallas import tpu as pltpu
from jax.sharding import Mesh
from jax.sharding import PartitionSpec as P

sharpness = 16.0
threshold = 0.3

AXES = ("z", "x", "y", "core")
PLANE = ("x", "y")
SIZES = {"z": 8, "x": 4, "y": 4, "core": 2}
DEPTH = SIZES["z"]
PEERS = SIZES["x"] * SIZES["y"]

DOCS = 192
HALF = DOCS // 2
E = 256
K = 64
COLUMNS = DEPTH * DOCS
ROWS = PEERS * DOCS
ROW_BLOCK = 512
COLUMN_BLOCK = 256
LANES = 128
PIVOTS = 4

bf16 = jnp.bfloat16
f32 = jnp.float32
HIGHEST = lax.Precision.HIGHEST


def shape(*dims, dtype=f32):
    return jax.ShapeDtypeStruct(dims, dtype)


def call(kernel, outs, args, scratch=(), flops=0):
    vmem = pl.BlockSpec(memory_space=pltpu.VMEM)
    moved = sum(math.prod(a.shape) * a.dtype.itemsize for a in (*args, *outs))
    return pl.pallas_call(
        kernel,
        out_shape=tuple(outs),
        in_specs=[vmem] * len(args),
        out_specs=tuple(vmem for _ in outs),
        scratch_shapes=list(scratch),
        cost_estimate=pl.CostEstimate(flops=flops, bytes_accessed=moved, transcendentals=0),
        compiler_params=pltpu.CompilerParams(vmem_limit_bytes=8 * 2**20),
    )(*args)


def left_lanes(value):
    return lax.broadcasted_iota(jnp.int32, value.shape, value.ndim - 1) < K


def swap_lanes(value):
    return pltpu.roll(value, K, value.ndim - 1)


def root_of(value):
    guess = lax.rsqrt(value)
    inv = guess * (1.5 - 0.5 * value * guess * guess)
    return inv, value * inv


def two_parts(value):
    hi = value.astype(bf16).astype(f32)
    return hi, (value - hi).astype(bf16).astype(f32)


def unit_kernel(emb_ref, plane_ref, depth_ref):
    wide = emb_ref[...].astype(f32)
    unit = wide * lax.rsqrt(jnp.sum(wide * wide, axis=1, keepdims=True) + 1e-06)
    unit = unit.astype(bf16)
    plane_ref[...] = jnp.broadcast_to((unit * (sharpness / 2))[None], plane_ref.shape)
    depth_ref[...] = jnp.broadcast_to(unit[None], depth_ref.shape)


def tile_kernel(last, *refs):
    if last:
        rows_ref, cols_ref, before_ref, start_ref, tile_ref, sums_ref, acc = refs
        acc[...] = before_ref[...]
    else:
        rows_ref, cols_ref, tile_ref, sums_ref, acc = refs
        acc[...] = jnp.zeros_like(acc)

    def block(i, _):
        at = pl.ds(pl.multiple_of(i * ROW_BLOCK, ROW_BLOCK), ROW_BLOCK)
        rows = rows_ref[at, :]
        for c in range(COLUMNS // COLUMN_BLOCK):
            where = slice(c * COLUMN_BLOCK, (c + 1) * COLUMN_BLOCK)
            scores = lax.dot_general(
                rows, cols_ref[where, :], (((1,), (1,)), ((), ())), preferred_element_type=f32
            )
            entry = 0.5 * jnp.tanh(scores - sharpness * threshold / 2) + 0.5
            tile_ref[at, where] = entry.astype(bf16)
            acc[:, where] += jnp.sum(entry.reshape(ROW_BLOCK // 8, 8, COLUMN_BLOCK), axis=0)
        return 0

    lax.fori_loop(0, ROWS // ROW_BLOCK, block, 0)
    if last:
        start = jnp.concatenate([start_ref[...], jnp.zeros((K, 2 * LANES - DOCS), f32)], axis=1)
        start = jnp.concatenate([start, jnp.zeros_like(start)], axis=0).T
        top, low = start[:HALF], swap_lanes(start[HALF:DOCS])
        sums_ref[:, :HALF, :] = jnp.broadcast_to((top + low)[None], (DEPTH, HALF, LANES))
        sums_ref[:, HALF:, :] = jnp.zeros((DEPTH, 16, LANES), f32)
        total = jnp.sum(acc[...], axis=0, keepdims=True)
        for k in range(COLUMNS // LANES):
            sums_ref[:, HALF + k : HALF + k + 1, :] = jnp.broadcast_to(
                total[None, :, k * LANES : (k + 1) * LANES], (DEPTH, 1, LANES)
            )
    else:
        sums_ref[...] = acc[...]


def multiply(tile_ref, weights_ref, out_ref, terms):
    chunks = 4

    def block(i, _):
        rows = chunks * DOCS
        sums = jnp.dot(
            tile_ref[pl.ds(pl.multiple_of(i * rows, rows), rows), :],
            weights_ref[...],
            preferred_element_type=f32,
        )
        for c in range(chunks):
            top = sums[c * DOCS : c * DOCS + HALF]
            low = sums[c * DOCS + HALF : (c + 1) * DOCS]
            out_ref[i * chunks + c, :HALF, :] = jnp.where(left_lanes(top), top, low)
            out_ref[i * chunks + c, HALF:, :] = terms
        return 0

    lax.fori_loop(0, PEERS // chunks, block, 0)


def rows_of(*values):
    index = lax.broadcasted_iota(jnp.int32, (8, LANES), 0)
    block = jnp.zeros((8, LANES), f32)
    for i, value in enumerate(values):
        block = jnp.where(index == i, jnp.broadcast_to(value, (8, LANES)), block)
    return block


def spread_lanes(packed):
    other = swap_lanes(packed)
    left = left_lanes(packed)
    return jnp.where(left, packed, other), jnp.where(left, other, packed)


def first_kernel(tile_ref, got_ref, out_ref, weights_ref, inv_ref, root_ref, all_inv, all_root):
    degree = jnp.sum(got_ref[:, HALF:, :], axis=0)
    blocks = COLUMNS // LANES
    degree = jnp.where(lax.broadcasted_iota(jnp.int32, degree.shape, 0) < blocks, degree, 1.0)
    tall = jnp.concatenate([degree, jnp.ones((LANES - degree.shape[0], LANES), f32)], axis=0).T
    inv, root = root_of(tall)
    total = jnp.zeros((1, LANES), f32)
    for k in range(blocks):
        at = slice(k * LANES, (k + 1) * LANES)
        all_inv[at, :] = jnp.broadcast_to(inv[:, k : k + 1], (LANES, LANES))
        all_root[at, :] = jnp.broadcast_to(root[:, k : k + 1], (LANES, LANES))
        total += jnp.sum(
            jnp.broadcast_to(tall[:, k : k + 1], (LANES, LANES)), axis=0, keepdims=True
        )
    correlation = jnp.zeros((1, LANES), f32)
    for j in range(DEPTH):
        for h, start in enumerate(spread_lanes(got_ref[j, :HALF, :])):
            at = slice(j * DOCS + h * HALF, j * DOCS + (h + 1) * HALF)
            weights_ref[at, :] = (all_inv[at, :] * start).astype(bf16)
            correlation += jnp.sum(all_root[at, :] * start, axis=0, keepdims=True)
    first = lax.axis_index("z") * DOCS
    top = pl.ds(pl.multiple_of(first, HALF), HALF)
    low = pl.ds(pl.multiple_of(first + HALF, HALF), HALF)
    for whole, own in ((all_inv, inv_ref), (all_root, root_ref)):
        upper = whole[top, :]
        own[...] = jnp.where(left_lanes(upper), upper, whole[low, :])
    multiply(tile_ref, weights_ref, out_ref, rows_of(correlation, total))


def second_kernel(tile_ref, got_ref, out_ref, weights_ref):
    terms = jnp.zeros((1, LANES), f32)
    for j in range(DEPTH):
        for h, weights in enumerate(spread_lanes(got_ref[j, :HALF, :].astype(f32))):
            at = slice(j * DOCS + h * HALF, j * DOCS + (h + 1) * HALF)
            weights_ref[at, :] = weights.astype(bf16)
        terms += jnp.sum(got_ref[j, HALF:, :].astype(f32), axis=0, keepdims=True)
    multiply(tile_ref, weights_ref, out_ref, rows_of(terms))


def again_kernel(tile_ref, weights_ref, other_ref, out_ref):
    multiply(tile_ref, weights_ref, out_ref, other_ref[0, HALF:, :])


def narrow_kernel(own_ref, other_ref, out_ref):
    out_ref[:, :HALF, :] = (own_ref[:, :HALF, :] + other_ref[:, :HALF, :]).astype(bf16)
    hi, mid = two_parts(own_ref[0, HALF:, :] + other_ref[0, HALF:, :])
    terms = jnp.concatenate([hi, mid], axis=0).astype(bf16)
    out_ref[:, HALF:, :] = jnp.broadcast_to(terms[None], (PEERS, 16, LANES))


def add_kernel(own_ref, other_ref, out_ref):
    out_ref[...] = own_ref[...] + other_ref[...]


def middle_kernel(got_ref, inv_ref, root_ref, out_ref, terms_ref):
    sums = jnp.sum(got_ref[:, :HALF, :].astype(f32), axis=0)
    terms = jnp.sum(got_ref[:, HALF:, :].astype(f32), axis=0)
    terms = terms[:8] + terms[8:]
    terms_ref[...] = terms
    inv, root = inv_ref[...], root_ref[...]
    vectors = inv * sums - root * (terms[0:1] / terms[1:2])
    out_ref[:, :HALF, :] = jnp.broadcast_to(
        (inv * vectors).astype(bf16)[None], (DEPTH, HALF, LANES)
    )
    correlation = jnp.sum(root * vectors, axis=0, keepdims=True)
    hi, mid = two_parts(correlation + swap_lanes(correlation))
    index = lax.broadcasted_iota(jnp.int32, (16, LANES), 0)
    terms = jnp.where(index == 0, hi, jnp.where(index == 1, mid, 0.0)).astype(bf16)
    out_ref[:, HALF:, :] = jnp.broadcast_to(terms[None], (DEPTH, 16, LANES))


def gram_kernel(got_ref, inv_ref, root_ref, terms_ref, vectors_ref, out_ref):
    sums = jnp.sum(got_ref[...], axis=0)
    ratio = sums[HALF : HALF + 1] / terms_ref[1:2, :]
    vectors = inv_ref[...] * sums[:HALF] - root_ref[...] * ratio
    vectors_ref[...] = vectors
    tall = jnp.concatenate([vectors, jnp.zeros((LANES - HALF, LANES), f32)], axis=0)
    product = jnp.dot(tall.T, tall, precision=HIGHEST, preferred_element_type=f32)
    gram = product[:K] + swap_lanes(product[K:])
    low = swap_lanes(gram[K // 2 :])
    gram = jnp.where(left_lanes(low), gram[: K // 2], low)
    out_ref[...] = jnp.broadcast_to(gram[None], out_ref.shape)


def fold_kernel(got_ref, out_ref):
    out_ref[...] = jnp.broadcast_to(jnp.sum(got_ref[...], axis=0)[None], out_ref.shape)


def solve_kernel(scale, got_ref, vectors_ref, out_ref):
    packed = jnp.sum(got_ref[...], axis=0)
    work = jnp.concatenate([packed, swap_lanes(packed)], axis=0)
    row = lax.broadcasted_iota(jnp.int32, (K, LANES), 0)
    lane = lax.broadcasted_iota(jnp.int32, (K, LANES), 1)
    work = jnp.where(lane < K, work, jnp.where(lane - K == row, 1.0, 0.0))
    tiles = [work[8 * t : 8 * t + 8] for t in range(K // 8)]
    index = lax.broadcasted_iota(jnp.int32, (8, LANES), 0)
    for k in range(0, K, PIVOTS):
        first, place = divmod(k, 8)
        rows = [tiles[first][place + i : place + i + 1] for i in range(PIVOTS)]
        inner = {
            (i, j): jnp.broadcast_to(rows[i][:, k + j : k + j + 1], (1, LANES))
            for i in range(PIVOTS)
            for j in range(i, PIVOTS)
        }
        after = range(first, K // 8)
        columns = [
            {t: jnp.broadcast_to(tiles[t][:, k + i : k + i + 1], (8, LANES)) for t in after}
            for i in range(PIVOTS)
        ]
        for i in range(PIVOTS):
            inverse = 1.0 / inner[i, i]
            for m in range(i + 1, PIVOTS):
                factor = inner[i, m] * inverse
                rows[m] = rows[m] - factor * rows[i]
                for j in range(m, PIVOTS):
                    inner[m, j] = inner[m, j] - factor * inner[i, j]
                for t in after:
                    columns[m][t] = columns[m][t] - columns[i][t] * factor
            pivot_row = rows[i] * inverse
            for t in after:
                column = columns[i][t]
                if t == first:
                    column = jnp.where(index > place + i, column, 0.0)
                tiles[t] = tiles[t] - column * pivot_row
    work = jnp.concatenate(tiles, axis=0)
    pivots = jnp.sum(jnp.where(lane == row, work, 0.0), axis=1, keepdims=True)
    inv, _ = root_of(pivots)
    right = jnp.where(lane < K, 0.0, work * (inv * scale))
    low = vectors_ref[...]
    padding = jnp.zeros((2 * LANES - DOCS, LANES), f32)
    vectors = jnp.concatenate([swap_lanes(low), low, padding], axis=0)
    out_ref[...] = lax.dot_general(
        right, vectors, (((1,), (1,)), ((), ())), precision=HIGHEST, preferred_element_type=f32
    )[:, :DOCS]


def exchange(value, axes):
    return lax.all_to_all(value, axes, 0, 0, tiled=True)


def swap_core(value):
    return lax.ppermute(value, "core", [(0, 1), (1, 0)])


def local(embeddings, start_vectors):
    all_docs = embeddings.shape[0] * lax.axis_size(AXES)
    plane, depth = call(
        unit_kernel,
        [shape(PEERS, DOCS, E, dtype=bf16), shape(DEPTH, DOCS, E, dtype=bf16)],
        [embeddings],
    )
    own_rows, depth = lax.optimization_barrier((exchange(plane, PLANE), depth))
    own_rows, columns = lax.optimization_barrier((own_rows, exchange(depth, ("z",))))
    own_rows = own_rows.reshape(ROWS, E)
    columns = columns.reshape(COLUMNS, E)
    other_rows = swap_core(own_rows)

    tile = shape(ROWS, COLUMNS, dtype=bf16)
    acc = pltpu.VMEM((8, COLUMNS), f32)
    flops = 2 * ROWS * COLUMNS * E
    own_tile, sums = call(
        functools.partial(tile_kernel, False),
        [tile, shape(8, COLUMNS)],
        [own_rows, columns],
        [acc],
        flops,
    )
    other_tile, sums = call(
        functools.partial(tile_kernel, True),
        [tile, shape(DEPTH, HALF + 16, LANES)],
        [other_rows, columns, sums, start_vectors.T],
        [acc],
        flops,
    )
    sums = exchange(sums, ("z",))

    flops = 2 * ROWS * COLUMNS * LANES
    sent = shape(PEERS, HALF + 8, LANES)
    weights = shape(COLUMNS, LANES, dtype=bf16)
    own = shape(HALF, LANES)
    spread = pltpu.VMEM((COLUMNS, LANES), f32)
    mine, packed, inv, root = call(
        first_kernel,
        [sent, weights, own, own],
        [other_tile, sums],
        [spread, spread],
        flops,
    )
    theirs = swap_core(mine)
    (mine,) = call(again_kernel, [sent], [own_tile, packed, mine], (), flops)
    (total,) = call(narrow_kernel, [shape(PEERS, HALF + 16, LANES, dtype=bf16)], [mine, theirs])
    got = exchange(total, PLANE)
    total, terms = call(
        middle_kernel,
        [shape(DEPTH, HALF + 16, LANES, dtype=bf16), shape(8, LANES)],
        [got, inv, root],
    )
    got = exchange(total, ("z",))
    mine, packed = call(second_kernel, [sent, weights], [other_tile, got], (), flops)
    theirs = swap_core(mine)
    (mine,) = call(again_kernel, [sent], [own_tile, packed, mine], (), flops)
    (total,) = call(add_kernel, [sent], [mine, theirs])
    got = exchange(total, PLANE)
    gram = shape(PEERS, K // 2, LANES)
    vectors, total = call(gram_kernel, [own, gram], [got, inv, root, terms])
    (total,) = call(fold_kernel, [gram], [exchange(total, ("z", "core"))])
    got = exchange(total, PLANE)
    (spectral,) = call(
        functools.partial(solve_kernel, math.sqrt(all_docs)), [shape(K, DOCS)], [got, vectors]
    )
    return spectral.T


def solution(mesh):
    fine = Mesh(mesh.devices.reshape(*SIZES.values()), AXES)
    return jax.shard_map(
        local,
        mesh=fine,
        in_specs=(P(AXES, None), P(AXES, None)),
        out_specs=P(AXES, None),
        check_vma=False,
    )
```

```python
import functools
import math

import jax
import jax.numpy as jnp
from jax import lax
from jax.experimental import pallas as pl
from jax.experimental.pallas import tpu as pltpu
from jax.sharding import Mesh
from jax.sharding import PartitionSpec as P

sharpness = 16.0
threshold = 0.3

AXES = ("zh", "zl", "x", "y", "core")
PLANE = ("x", "y")
LINE = ("zl", "zh")
SIZES = {"zh": 4, "zl": 2, "x": 4, "y": 4, "core": 2}
DEPTH = SIZES["zh"] * SIZES["zl"]
PEERS = SIZES["x"] * SIZES["y"]

DOCS = 192
HALF = DOCS // 2
E = 256
K = 64
COLUMNS = DEPTH * DOCS
ROWS = PEERS * DOCS
ROW_BLOCK = 512
COLUMN_BLOCK = 256
LANES = 128
PIVOTS = 4

bf16 = jnp.bfloat16
f32 = jnp.float32
HIGHEST = lax.Precision.HIGHEST


def shape(*dims, dtype=f32):
    return jax.ShapeDtypeStruct(dims, dtype)


def call(kernel, outs, args, scratch=(), flops=0):
    vmem = pl.BlockSpec(memory_space=pltpu.VMEM)
    moved = sum(math.prod(a.shape) * a.dtype.itemsize for a in (*args, *outs))
    return pl.pallas_call(
        kernel,
        out_shape=tuple(outs),
        in_specs=[vmem] * len(args),
        out_specs=tuple(vmem for _ in outs),
        scratch_shapes=list(scratch),
        cost_estimate=pl.CostEstimate(flops=flops, bytes_accessed=moved, transcendentals=0),
        compiler_params=pltpu.CompilerParams(vmem_limit_bytes=8 * 2**20),
    )(*args)


def left_lanes(value):
    return lax.broadcasted_iota(jnp.int32, value.shape, value.ndim - 1) < K


def swap_lanes(value):
    return pltpu.roll(value, K, value.ndim - 1)


def root_of(value):
    guess = lax.rsqrt(value)
    inv = guess * (1.5 - 0.5 * value * guess * guess)
    return inv, value * inv


def two_parts(value):
    hi = value.astype(bf16).astype(f32)
    return hi, (value - hi).astype(bf16).astype(f32)


def unit_kernel(emb_ref, start_ref, plane_ref, line_ref):
    wide = emb_ref[...].astype(f32)
    unit = wide * lax.rsqrt(jnp.sum(wide * wide, axis=1, keepdims=True) + 1e-06)
    unit = unit.astype(bf16)
    plane_ref[...] = jnp.broadcast_to((unit * (sharpness / 2))[None], plane_ref.shape)
    line_ref[:, :, :E] = jnp.broadcast_to(unit[None], (SIZES["zh"], DOCS, E))
    start = jnp.concatenate([start_ref[...], jnp.zeros((K, 2 * LANES - DOCS), f32)], axis=1)
    start = jnp.concatenate([start, jnp.zeros_like(start)], axis=0).T[:DOCS]
    hi, mid = two_parts(start)
    pair = jnp.where(left_lanes(hi), hi, swap_lanes(mid)).astype(bf16)
    line_ref[:, :, E:] = jnp.broadcast_to(pair[None], (SIZES["zh"], DOCS, 2 * K))


def tile_kernel(last, *refs):
    if last:
        rows_ref, cols_ref, before_ref, tile_ref, sums_ref, acc = refs
        acc[...] = before_ref[...]
    else:
        rows_ref, same_ref, other_ref, tile_ref, sums_ref, cols_ref, acc = refs
        acc[...] = jnp.zeros_like(acc)
        side = lax.axis_index("zl") * (COLUMNS // 2)
        cols_ref[pl.ds(pl.multiple_of(side, COLUMNS // 2), COLUMNS // 2), :] = same_ref[...]
        side = COLUMNS // 2 - side
        cols_ref[pl.ds(pl.multiple_of(side, COLUMNS // 2), COLUMNS // 2), :] = other_ref[...]

    def block(i, _):
        at = pl.ds(pl.multiple_of(i * ROW_BLOCK, ROW_BLOCK), ROW_BLOCK)
        rows = rows_ref[at, :]
        for c in range(COLUMNS // COLUMN_BLOCK):
            where = slice(c * COLUMN_BLOCK, (c + 1) * COLUMN_BLOCK)
            scores = lax.dot_general(
                rows, cols_ref[where, :E], (((1,), (1,)), ((), ())), preferred_element_type=f32
            )
            entry = jnp.tanh(scores - sharpness * threshold / 2) + 1.0
            tile_ref[at, where] = entry.astype(bf16)
            acc[:, where] += jnp.sum(entry.reshape(ROW_BLOCK // 8, 8, COLUMN_BLOCK), axis=0)
        return 0

    lax.fori_loop(0, ROWS // ROW_BLOCK, block, 0)
    if last:
        total = 0.5 * jnp.sum(acc[...], axis=0, keepdims=True)
        sums_ref[...] = jnp.zeros_like(sums_ref)
        for k in range(COLUMNS // LANES):
            sums_ref[:, k : k + 1, :] = jnp.broadcast_to(
                total[None, :, k * LANES : (k + 1) * LANES], (DEPTH, 1, LANES)
            )
    else:
        sums_ref[...] = acc[...]


def multiply(tile_ref, weights_ref, out_ref, terms):
    chunks = 8

    def block(i, _):
        rows = chunks * DOCS
        sums = jnp.dot(
            tile_ref[pl.ds(pl.multiple_of(i * rows, rows), rows), :],
            weights_ref[...],
            preferred_element_type=f32,
        )
        for c in range(chunks):
            top = sums[c * DOCS : c * DOCS + HALF]
            low = sums[c * DOCS + HALF : (c + 1) * DOCS]
            out_ref[i * chunks + c, :HALF, :] = jnp.where(left_lanes(top), top, low)
            out_ref[i * chunks + c, HALF:, :] = terms
        return 0

    lax.fori_loop(0, PEERS // chunks, block, 0)


def rows_of(*values):
    index = lax.broadcasted_iota(jnp.int32, (8, LANES), 0)
    block = jnp.zeros((8, LANES), f32)
    for i, value in enumerate(values):
        block = jnp.where(index == i, jnp.broadcast_to(value, (8, LANES)), block)
    return block


def spread_lanes(packed):
    other = swap_lanes(packed)
    left = left_lanes(packed)
    return jnp.where(left, packed, other), jnp.where(left, other, packed)


def first_kernel(
    tile_ref, sums_ref, cols_ref, out_ref, weights_ref, inv_ref, root_ref, all_inv, all_root
):
    degree = jnp.sum(sums_ref[...], axis=0)
    blocks = COLUMNS // LANES
    degree = jnp.where(lax.broadcasted_iota(jnp.int32, degree.shape, 0) < blocks, degree, 1.0)
    tall = jnp.concatenate([degree, jnp.ones((LANES - degree.shape[0], LANES), f32)], axis=0).T
    inv, root = root_of(tall)
    correlation = jnp.zeros((1, LANES), f32)
    total = jnp.zeros((1, LANES), f32)
    for k in range(blocks):
        at = slice(k * LANES, (k + 1) * LANES)
        pair = cols_ref[at, E:].astype(f32)
        start = pair + swap_lanes(pair)
        own_inv = jnp.broadcast_to(inv[:, k : k + 1], (LANES, LANES))
        own_root = jnp.broadcast_to(root[:, k : k + 1], (LANES, LANES))
        all_inv[at, :] = own_inv
        all_root[at, :] = own_root
        weights_ref[at, :] = (0.5 * own_inv * start).astype(bf16)
        correlation += jnp.sum(own_root * start, axis=0, keepdims=True)
        total += jnp.sum(
            jnp.broadcast_to(tall[:, k : k + 1], (LANES, LANES)), axis=0, keepdims=True
        )
    first = (lax.axis_index("zl") * SIZES["zh"] + lax.axis_index("zh")) * DOCS
    top = pl.ds(pl.multiple_of(first, HALF), HALF)
    low = pl.ds(pl.multiple_of(first + HALF, HALF), HALF)
    for whole, own in ((all_inv, inv_ref), (all_root, root_ref)):
        upper = whole[top, :]
        own[...] = jnp.where(left_lanes(upper), upper, whole[low, :])
    multiply(tile_ref, weights_ref, out_ref, rows_of(correlation, total))


def second_kernel(tile_ref, got_ref, out_ref, weights_ref):
    terms = jnp.zeros((1, LANES), f32)
    for j in range(DEPTH):
        for h, weights in enumerate(spread_lanes(got_ref[j, :HALF, :].astype(f32))):
            at = slice(j * DOCS + h * HALF, j * DOCS + (h + 1) * HALF)
            weights_ref[at, :] = weights.astype(bf16)
        terms += jnp.sum(got_ref[j, HALF:, :].astype(f32), axis=0, keepdims=True)
    multiply(tile_ref, weights_ref, out_ref, rows_of(terms))


def again_kernel(tile_ref, weights_ref, other_ref, out_ref):
    multiply(tile_ref, weights_ref, out_ref, other_ref[0, HALF:, :])


def narrow_kernel(own_ref, other_ref, out_ref):
    out_ref[:, :HALF, :] = (own_ref[:, :HALF, :] + other_ref[:, :HALF, :]).astype(bf16)
    hi, mid = two_parts(own_ref[0, HALF:, :] + other_ref[0, HALF:, :])
    terms = jnp.concatenate([hi, mid], axis=0).astype(bf16)
    out_ref[:, HALF:, :] = jnp.broadcast_to(terms[None], (PEERS, 16, LANES))


def add_kernel(own_ref, other_ref, out_ref):
    out_ref[...] = own_ref[...] + other_ref[...]


def middle_kernel(got_ref, inv_ref, root_ref, out_ref, terms_ref):
    sums = jnp.sum(got_ref[:, :HALF, :].astype(f32), axis=0)
    terms = jnp.sum(got_ref[:, HALF:, :].astype(f32), axis=0)
    terms = terms[:8] + terms[8:]
    terms_ref[...] = terms
    inv, root = inv_ref[...], root_ref[...]
    vectors = inv * sums - root * (terms[0:1] / terms[1:2])
    out_ref[:, :HALF, :] = jnp.broadcast_to(
        (0.5 * inv * vectors).astype(bf16)[None], (DEPTH, HALF, LANES)
    )
    correlation = jnp.sum(root * vectors, axis=0, keepdims=True)
    hi, mid = two_parts(correlation + swap_lanes(correlation))
    index = lax.broadcasted_iota(jnp.int32, (16, LANES), 0)
    terms = jnp.where(index == 0, hi, jnp.where(index == 1, mid, 0.0)).astype(bf16)
    out_ref[:, HALF:, :] = jnp.broadcast_to(terms[None], (DEPTH, 16, LANES))


def gram_kernel(got_ref, inv_ref, root_ref, terms_ref, vectors_ref, out_ref):
    sums = jnp.sum(got_ref[...], axis=0)
    ratio = sums[HALF : HALF + 1] / terms_ref[1:2, :]
    vectors = inv_ref[...] * sums[:HALF] - root_ref[...] * ratio
    vectors_ref[...] = vectors
    tall = jnp.concatenate([vectors, jnp.zeros((LANES - HALF, LANES), f32)], axis=0)
    product = jnp.dot(tall.T, tall, precision=HIGHEST, preferred_element_type=f32)
    gram = product[:K] + swap_lanes(product[K:])
    low = swap_lanes(gram[K // 2 :])
    gram = jnp.where(left_lanes(low), gram[: K // 2], low)
    out_ref[...] = jnp.broadcast_to(gram[None], out_ref.shape)


def fold_kernel(got_ref, out_ref):
    out_ref[...] = jnp.broadcast_to(jnp.sum(got_ref[...], axis=0)[None], out_ref.shape)


def solve_kernel(scale, got_ref, vectors_ref, out_ref):
    packed = jnp.sum(got_ref[...], axis=0)
    work = jnp.concatenate([packed, swap_lanes(packed)], axis=0)
    row = lax.broadcasted_iota(jnp.int32, (K, LANES), 0)
    lane = lax.broadcasted_iota(jnp.int32, (K, LANES), 1)
    work = jnp.where(lane < K, work, jnp.where(lane - K == row, 1.0, 0.0))
    tiles = [work[8 * t : 8 * t + 8] for t in range(K // 8)]
    index = lax.broadcasted_iota(jnp.int32, (8, LANES), 0)
    for k in range(0, K, PIVOTS):
        first, place = divmod(k, 8)
        rows = [tiles[first][place + i : place + i + 1] for i in range(PIVOTS)]
        inner = {
            (i, j): jnp.broadcast_to(rows[i][:, k + j : k + j + 1], (1, LANES))
            for i in range(PIVOTS)
            for j in range(i, PIVOTS)
        }
        after = range(first, K // 8)
        columns = [
            {t: jnp.broadcast_to(tiles[t][:, k + i : k + i + 1], (8, LANES)) for t in after}
            for i in range(PIVOTS)
        ]
        for i in range(PIVOTS):
            inverse = 1.0 / inner[i, i]
            for m in range(i + 1, PIVOTS):
                factor = inner[i, m] * inverse
                rows[m] = rows[m] - factor * rows[i]
                for j in range(m, PIVOTS):
                    inner[m, j] = inner[m, j] - factor * inner[i, j]
                for t in after:
                    columns[m][t] = columns[m][t] - columns[i][t] * factor
            pivot_row = rows[i] * inverse
            for t in after:
                column = columns[i][t]
                if t == first:
                    column = jnp.where(index > place + i, column, 0.0)
                tiles[t] = tiles[t] - column * pivot_row
    work = jnp.concatenate(tiles, axis=0)
    pivots = jnp.sum(jnp.where(lane == row, work, 0.0), axis=1, keepdims=True)
    inv, _ = root_of(pivots)
    right = jnp.where(lane < K, 0.0, work * (inv * scale))
    low = vectors_ref[...]
    padding = jnp.zeros((2 * LANES - DOCS, LANES), f32)
    vectors = jnp.concatenate([swap_lanes(low), low, padding], axis=0)
    out_ref[...] = lax.dot_general(
        right, vectors, (((1,), (1,)), ((), ())), precision=HIGHEST, preferred_element_type=f32
    )[:, :DOCS]


def exchange(value, axes):
    return lax.all_to_all(value, axes, 0, 0, tiled=True)


def swap_core(value):
    return lax.ppermute(value, "core", [(0, 1), (1, 0)])


def local(embeddings, start_vectors):
    all_docs = embeddings.shape[0] * lax.axis_size(AXES)
    width = E + 2 * K
    plane, line = call(
        unit_kernel,
        [shape(PEERS, DOCS, E, dtype=bf16), shape(SIZES["zh"], DOCS, width, dtype=bf16)],
        [embeddings, start_vectors.T],
    )
    same, plane = lax.optimization_barrier((exchange(line, ("zh",)), plane))
    same = same.reshape(COLUMNS // 2, width)
    other = lax.ppermute(same, "zl", [(0, 1), (1, 0)])
    own_rows, other = lax.optimization_barrier((exchange(plane, PLANE), other))
    own_rows = own_rows.reshape(ROWS, E)
    other_rows = swap_core(own_rows)

    tile = shape(ROWS, COLUMNS, dtype=bf16)
    acc = pltpu.VMEM((8, COLUMNS), f32)
    flops = 2 * ROWS * COLUMNS * E
    own_tile, sums, columns = call(
        functools.partial(tile_kernel, False),
        [tile, shape(8, COLUMNS), shape(COLUMNS, width, dtype=bf16)],
        [own_rows, same, other],
        [acc],
        flops,
    )
    other_tile, sums = call(
        functools.partial(tile_kernel, True),
        [tile, shape(DEPTH, 16, LANES)],
        [other_rows, columns, sums],
        [acc],
        flops,
    )
    sums = exchange(sums, LINE)

    flops = 2 * ROWS * COLUMNS * LANES
    sent = shape(PEERS, HALF + 8, LANES)
    weights = shape(COLUMNS, LANES, dtype=bf16)
    own = shape(HALF, LANES)
    spread = pltpu.VMEM((COLUMNS, LANES), f32)
    mine, packed, inv, root = call(
        first_kernel,
        [sent, weights, own, own],
        [other_tile, sums, columns],
        [spread, spread],
        flops,
    )
    theirs = swap_core(mine)
    (mine,) = call(again_kernel, [sent], [own_tile, packed, mine], (), flops)
    (total,) = call(narrow_kernel, [shape(PEERS, HALF + 16, LANES, dtype=bf16)], [mine, theirs])
    got = exchange(total, PLANE)
    total, terms = call(
        middle_kernel,
        [shape(DEPTH, HALF + 16, LANES, dtype=bf16), shape(8, LANES)],
        [got, inv, root],
    )
    got = exchange(total, LINE)
    mine, packed = call(second_kernel, [sent, weights], [other_tile, got], (), flops)
    theirs = swap_core(mine)
    (mine,) = call(again_kernel, [sent], [own_tile, packed, mine], (), flops)
    (total,) = call(add_kernel, [sent], [mine, theirs])
    got = exchange(total, PLANE)
    gram = shape(PEERS, K // 2, LANES)
    vectors, total = call(gram_kernel, [own, gram], [got, inv, root, terms])
    (total,) = call(fold_kernel, [gram], [exchange(total, (*LINE, "core"))])
    got = exchange(total, PLANE)
    (spectral,) = call(
        functools.partial(solve_kernel, math.sqrt(all_docs)), [shape(K, DOCS)], [got, vectors]
    )
    return spectral.T


def solution(mesh):
    fine = Mesh(mesh.devices.reshape(*SIZES.values()), AXES)
    return jax.shard_map(
        local,
        mesh=fine,
        in_specs=(P(AXES, None), P(AXES, None)),
        out_specs=P(AXES, None),
        check_vma=False,
    )
```

```python
import functools
import math

import jax
import jax.numpy as jnp
from jax import lax
from jax.experimental import pallas as pl
from jax.experimental.pallas import tpu as pltpu
from jax.sharding import Mesh
from jax.sharding import PartitionSpec as P

sharpness = 16.0
threshold = 0.3

AXES = ("zh", "zl", "x", "y", "core")
PLANE = ("x", "y")
LINE = ("zl", "zh")
SIZES = {"zh": 4, "zl": 2, "x": 4, "y": 4, "core": 2}
DEPTH = SIZES["zh"] * SIZES["zl"]
PEERS = SIZES["x"] * SIZES["y"]

DOCS = 192
HALF = DOCS // 2
E = 256
K = 64
COLUMNS = DEPTH * DOCS
ROWS = PEERS * DOCS
ROW_BLOCK = 3072
COLUMN_BLOCK = 256
LANES = 128
PIVOTS = 8

bf16 = jnp.bfloat16
f32 = jnp.float32
HIGHEST = lax.Precision.HIGHEST


def shape(*dims, dtype=f32):
    return jax.ShapeDtypeStruct(dims, dtype)


def call(kernel, outs, args, scratch=(), flops=0):
    vmem = pl.BlockSpec(memory_space=pltpu.VMEM)
    moved = sum(math.prod(a.shape) * a.dtype.itemsize for a in (*args, *outs))
    return pl.pallas_call(
        kernel,
        out_shape=tuple(outs),
        in_specs=[vmem] * len(args),
        out_specs=tuple(vmem for _ in outs),
        scratch_shapes=list(scratch),
        cost_estimate=pl.CostEstimate(flops=flops, bytes_accessed=moved, transcendentals=0),
        compiler_params=pltpu.CompilerParams(vmem_limit_bytes=8 * 2**20),
    )(*args)


def left_lanes(value):
    return lax.broadcasted_iota(jnp.int32, value.shape, value.ndim - 1) < K


def swap_lanes(value):
    return pltpu.roll(value, K, value.ndim - 1)


def root_of(value):
    guess = lax.rsqrt(value)
    inv = guess * (1.5 - 0.5 * value * guess * guess)
    return inv, value * inv


def two_parts(value):
    hi = value.astype(bf16).astype(f32)
    return hi, (value - hi).astype(bf16).astype(f32)


def unit_kernel(emb_ref, line_ref):
    wide = emb_ref[...].astype(f32)
    unit = wide * lax.rsqrt(jnp.sum(wide * wide, axis=1, keepdims=True) + 1e-06)
    line_ref[...] = jnp.broadcast_to(unit.astype(bf16)[None], line_ref.shape)


def plane_kernel(line_ref, plane_ref):
    plane_ref[...] = jnp.broadcast_to((line_ref[0] * (sharpness / 2))[None], plane_ref.shape)


def pack_kernel(start_ref, out_ref):
    start = jnp.concatenate([start_ref[...], jnp.zeros((K, 2 * LANES - DOCS), f32)], axis=1)
    start = jnp.concatenate([start, jnp.zeros_like(start)], axis=0).T
    out_ref[0] = start[:HALF] + swap_lanes(start[HALF:DOCS])


def tile_kernel(last, *refs):
    if last:
        rows_ref, cols_ref, before_ref, tile_ref, sums_ref, acc = refs
        acc[...] = before_ref[...]
    else:
        rows_ref, same_ref, other_ref, tile_ref, sums_ref, cols_ref, acc = refs
        acc[...] = jnp.zeros_like(acc)
        side = lax.axis_index("zl") * (COLUMNS // 2)
        cols_ref[pl.ds(pl.multiple_of(side, COLUMNS // 2), COLUMNS // 2), :] = same_ref[...]
        side = COLUMNS // 2 - side
        cols_ref[pl.ds(pl.multiple_of(side, COLUMNS // 2), COLUMNS // 2), :] = other_ref[...]

    def block(i, _):
        at = pl.ds(pl.multiple_of(i * ROW_BLOCK, ROW_BLOCK), ROW_BLOCK)
        rows = rows_ref[at, :]
        for c in range(COLUMNS // COLUMN_BLOCK):
            where = slice(c * COLUMN_BLOCK, (c + 1) * COLUMN_BLOCK)
            scores = lax.dot_general(
                rows, cols_ref[where, :], (((1,), (1,)), ((), ())), preferred_element_type=f32
            )
            entry = jnp.tanh(scores - sharpness * threshold / 2) + 1.0
            tile_ref[at, where] = entry.astype(bf16)
            acc[:, where] += jnp.sum(entry.reshape(ROW_BLOCK // 8, 8, COLUMN_BLOCK), axis=0)
        return 0

    lax.fori_loop(0, ROWS // ROW_BLOCK, block, 0)
    if last:
        total = 0.5 * jnp.sum(acc[...], axis=0, keepdims=True)
        sums_ref[...] = jnp.zeros_like(sums_ref)
        for k in range(COLUMNS // LANES):
            sums_ref[:, k : k + 1, :] = jnp.broadcast_to(
                total[None, :, k * LANES : (k + 1) * LANES], (DEPTH, 1, LANES)
            )
    else:
        sums_ref[...] = acc[...]


def multiply(tile_ref, weights_ref, out_ref, terms):
    chunks = 16

    def block(i, _):
        rows = chunks * DOCS
        sums = jnp.dot(
            tile_ref[pl.ds(pl.multiple_of(i * rows, rows), rows), :],
            weights_ref[...],
            preferred_element_type=f32,
        )
        for c in range(chunks):
            top = sums[c * DOCS : c * DOCS + HALF]
            low = sums[c * DOCS + HALF : (c + 1) * DOCS]
            out_ref[i * chunks + c, :HALF, :] = jnp.where(left_lanes(top), top, low)
            out_ref[i * chunks + c, HALF:, :] = terms
        return 0

    lax.fori_loop(0, PEERS // chunks, block, 0)


def rows_of(*values):
    index = lax.broadcasted_iota(jnp.int32, (8, LANES), 0)
    block = jnp.zeros((8, LANES), f32)
    for i, value in enumerate(values):
        block = jnp.where(index == i, jnp.broadcast_to(value, (8, LANES)), block)
    return block


def spread_lanes(packed):
    other = swap_lanes(packed)
    left = left_lanes(packed)
    return jnp.where(left, packed, other), jnp.where(left, other, packed)


def spread_lanes(packed):
    other = swap_lanes(packed)
    left = left_lanes(packed)
    return jnp.where(left, packed, other), jnp.where(left, other, packed)


def first_kernel(
    tile_ref, sums_ref, cols_ref, out_ref, weights_ref, inv_ref, root_ref, all_inv, all_root
):
    degree = jnp.sum(sums_ref[...], axis=0)
    blocks = COLUMNS // LANES
    degree = jnp.where(lax.broadcasted_iota(jnp.int32, degree.shape, 0) < blocks, degree, 1.0)
    tall = jnp.concatenate([degree, jnp.ones((LANES - degree.shape[0], LANES), f32)], axis=0).T
    inv, root = root_of(tall)
    correlation = jnp.zeros((1, LANES), f32)
    total = jnp.zeros((1, LANES), f32)
    for k in range(blocks):
        at = slice(k * LANES, (k + 1) * LANES)
        pair = cols_ref[at, E:].astype(f32)
        start = pair + swap_lanes(pair)
        own_inv = jnp.broadcast_to(inv[:, k : k + 1], (LANES, LANES))
        own_root = jnp.broadcast_to(root[:, k : k + 1], (LANES, LANES))
        all_inv[at, :] = own_inv
        all_root[at, :] = own_root
        weights_ref[at, :] = (0.5 * own_inv * start).astype(bf16)
        correlation += jnp.sum(own_root * start, axis=0, keepdims=True)
        total += jnp.sum(
            jnp.broadcast_to(tall[:, k : k + 1], (LANES, LANES)), axis=0, keepdims=True
        )
    first = (lax.axis_index("zl") * SIZES["zh"] + lax.axis_index("zh")) * DOCS
    top = pl.ds(pl.multiple_of(first, HALF), HALF)
    low = pl.ds(pl.multiple_of(first + HALF, HALF), HALF)
    for whole, own in ((all_inv, inv_ref), (all_root, root_ref)):
        upper = whole[top, :]
        own[...] = jnp.where(left_lanes(upper), upper, whole[low, :])
    multiply(tile_ref, weights_ref, out_ref, rows_of(correlation, total))


def first_kernel(
    tile_ref,
    sums_ref,
    same_ref,
    other_ref,
    out_ref,
    weights_ref,
    inv_ref,
    root_ref,
    all_inv,
    all_root,
):
    degree = jnp.sum(sums_ref[...], axis=0)
    blocks = COLUMNS // LANES
    degree = jnp.where(lax.broadcasted_iota(jnp.int32, degree.shape, 0) < blocks, degree, 1.0)
    tall = jnp.concatenate([degree, jnp.ones((LANES - degree.shape[0], LANES), f32)], axis=0).T
    inv, root = root_of(tall)
    total = jnp.zeros((1, LANES), f32)
    for k in range(blocks):
        at = slice(k * LANES, (k + 1) * LANES)
        all_inv[at, :] = jnp.broadcast_to(inv[:, k : k + 1], (LANES, LANES))
        all_root[at, :] = jnp.broadcast_to(root[:, k : k + 1], (LANES, LANES))
        total += jnp.sum(
            jnp.broadcast_to(tall[:, k : k + 1], (LANES, LANES)), axis=0, keepdims=True
        )
    zh, zl = lax.axis_index("zh"), lax.axis_index("zl")
    correlation = jnp.zeros((1, LANES), f32)
    for side, start_ref in ((zl, same_ref), (1 - zl, other_ref)):
        for j, flip in enumerate((0, 2, 1, 3)):
            first = (side * SIZES["zh"] + jnp.bitwise_xor(zh, flip)) * DOCS
            for h, start in enumerate(spread_lanes(start_ref[j])):
                at = pl.ds(pl.multiple_of(first + h * HALF, HALF), HALF)
                weights_ref[at, :] = (0.5 * all_inv[at, :] * start).astype(bf16)
                correlation += jnp.sum(all_root[at, :] * start, axis=0, keepdims=True)
    first = (zl * SIZES["zh"] + zh) * DOCS
    top = pl.ds(pl.multiple_of(first, HALF), HALF)
    low = pl.ds(pl.multiple_of(first + HALF, HALF), HALF)
    for whole, own in ((all_inv, inv_ref), (all_root, root_ref)):
        upper = whole[top, :]
        own[...] = jnp.where(left_lanes(upper), upper, whole[low, :])
    multiply(tile_ref, weights_ref, out_ref, rows_of(correlation, total))


def second_kernel(tile_ref, got_ref, out_ref, weights_ref):
    terms = jnp.zeros((1, LANES), f32)
    for j in range(DEPTH):
        for h, weights in enumerate(spread_lanes(got_ref[j, :HALF, :].astype(f32))):
            at = slice(j * DOCS + h * HALF, j * DOCS + (h + 1) * HALF)
            weights_ref[at, :] = weights.astype(bf16)
        terms += jnp.sum(got_ref[j, HALF:, :].astype(f32), axis=0, keepdims=True)
    multiply(tile_ref, weights_ref, out_ref, rows_of(terms))


def again_kernel(tile_ref, weights_ref, other_ref, out_ref):
    multiply(tile_ref, weights_ref, out_ref, other_ref[0, HALF:, :])


def narrow_kernel(own_ref, other_ref, out_ref):
    out_ref[:, :HALF, :] = (own_ref[:, :HALF, :] + other_ref[:, :HALF, :]).astype(bf16)
    hi, mid = two_parts(own_ref[0, HALF:, :] + other_ref[0, HALF:, :])
    terms = jnp.concatenate([hi, mid], axis=0).astype(bf16)
    out_ref[:, HALF:, :] = jnp.broadcast_to(terms[None], (PEERS, 16, LANES))


def add_kernel(own_ref, other_ref, out_ref):
    out_ref[...] = own_ref[...] + other_ref[...]


def middle_kernel(got_ref, inv_ref, root_ref, out_ref, terms_ref):
    sums = jnp.sum(got_ref[:, :HALF, :].astype(f32), axis=0)
    terms = jnp.sum(got_ref[:, HALF:, :].astype(f32), axis=0)
    terms = terms[:8] + terms[8:]
    terms_ref[...] = terms
    inv, root = inv_ref[...], root_ref[...]
    vectors = inv * sums - root * (terms[0:1] / terms[1:2])
    out_ref[:, :HALF, :] = jnp.broadcast_to(
        (0.5 * inv * vectors).astype(bf16)[None], (DEPTH, HALF, LANES)
    )
    correlation = jnp.sum(root * vectors, axis=0, keepdims=True)
    hi, mid = two_parts(correlation + swap_lanes(correlation))
    index = lax.broadcasted_iota(jnp.int32, (16, LANES), 0)
    terms = jnp.where(index == 0, hi, jnp.where(index == 1, mid, 0.0)).astype(bf16)
    out_ref[:, HALF:, :] = jnp.broadcast_to(terms[None], (DEPTH, 16, LANES))


def gram_kernel(got_ref, inv_ref, root_ref, terms_ref, vectors_ref, out_ref):
    sums = jnp.sum(got_ref[...], axis=0)
    ratio = sums[HALF : HALF + 1] / terms_ref[1:2, :]
    vectors = inv_ref[...] * sums[:HALF] - root_ref[...] * ratio
    vectors_ref[...] = vectors
    tall = jnp.concatenate([vectors, jnp.zeros((LANES - HALF, LANES), f32)], axis=0)
    product = jnp.dot(tall.T, tall, precision=HIGHEST, preferred_element_type=f32)
    gram = product[:K] + swap_lanes(product[K:])
    low = swap_lanes(gram[K // 2 :])
    gram = jnp.where(left_lanes(low), gram[: K // 2], low)
    out_ref[...] = jnp.broadcast_to(gram[None], out_ref.shape)


def fold_kernel(got_ref, out_ref):
    out_ref[...] = jnp.broadcast_to(jnp.sum(got_ref[...], axis=0)[None], out_ref.shape)


def solve_kernel(scale, got_ref, vectors_ref, out_ref):
    packed = jnp.sum(got_ref[...], axis=0)
    work = jnp.concatenate([packed, swap_lanes(packed)], axis=0)
    row = lax.broadcasted_iota(jnp.int32, (K, LANES), 0)
    lane = lax.broadcasted_iota(jnp.int32, (K, LANES), 1)
    work = jnp.where(lane < K, work, jnp.where(lane - K == row, 1.0, 0.0))
    tiles = [work[8 * t : 8 * t + 8] for t in range(K // 8)]
    index = lax.broadcasted_iota(jnp.int32, (8, LANES), 0)
    for k in range(0, K, PIVOTS):
        first, place = divmod(k, 8)
        rows = [tiles[first][place + i : place + i + 1] for i in range(PIVOTS)]
        inner = {
            (i, j): jnp.broadcast_to(rows[i][:, k + j : k + j + 1], (1, LANES))
            for i in range(PIVOTS)
            for j in range(i, PIVOTS)
        }
        after = range(first, K // 8)
        columns = [
            {t: jnp.broadcast_to(tiles[t][:, k + i : k + i + 1], (8, LANES)) for t in after}
            for i in range(PIVOTS)
        ]
        for i in range(PIVOTS):
            inverse = 1.0 / inner[i, i]
            for m in range(i + 1, PIVOTS):
                factor = inner[i, m] * inverse
                rows[m] = rows[m] - factor * rows[i]
                for j in range(m, PIVOTS):
                    inner[m, j] = inner[m, j] - factor * inner[i, j]
                for t in after:
                    columns[m][t] = columns[m][t] - columns[i][t] * factor
            pivot_row = rows[i] * inverse
            for t in after:
                column = columns[i][t]
                if t == first:
                    column = jnp.where(index > place + i, column, 0.0)
                tiles[t] = tiles[t] - column * pivot_row
    work = jnp.concatenate(tiles, axis=0)
    pivots = jnp.sum(jnp.where(lane == row, work, 0.0), axis=1, keepdims=True)
    inv, _ = root_of(pivots)
    right = jnp.where(lane < K, 0.0, work * (inv * scale))
    low = vectors_ref[...]
    padding = jnp.zeros((2 * LANES - DOCS, LANES), f32)
    vectors = jnp.concatenate([swap_lanes(low), low, padding], axis=0)
    out_ref[...] = lax.dot_general(
        right, vectors, (((1,), (1,)), ((), ())), precision=HIGHEST, preferred_element_type=f32
    )[:, :DOCS]


def exchange(value, axes):
    return lax.all_to_all(value, axes, 0, 0, tiled=True)


def flip(value, axis, bits):
    return lax.ppermute(value, axis, [(i, i ^ bits) for i in range(SIZES[axis])])


def local(embeddings, start_vectors):
    all_docs = embeddings.shape[0] * lax.axis_size(AXES)
    (line,) = call(unit_kernel, [shape(SIZES["zh"], DOCS, E, dtype=bf16)], [embeddings])
    (plane,) = call(plane_kernel, [shape(PEERS, DOCS, E, dtype=bf16)], [line])
    (start,) = call(pack_kernel, [shape(1, HALF, LANES)], [start_vectors.T])
    same, plane, start = lax.optimization_barrier((exchange(line, ("zh",)), plane, start))
    same = same.reshape(COLUMNS // 2, E)
    other = flip(same, "zl", 1)
    start = jnp.concatenate([start, flip(start, "zh", 2)], axis=0)
    start = jnp.concatenate([start, flip(start, "zh", 1)], axis=0)
    own_rows, other, start = lax.optimization_barrier((exchange(plane, PLANE), other, start))
    other_start = flip(start, "zl", 1)
    own_rows = own_rows.reshape(ROWS, E)
    other_rows = flip(own_rows, "core", 1)

    tile = shape(ROWS, COLUMNS, dtype=bf16)
    acc = pltpu.VMEM((8, COLUMNS), f32)
    flops = 2 * ROWS * COLUMNS * E
    own_tile, sums, columns = call(
        functools.partial(tile_kernel, False),
        [tile, shape(8, COLUMNS), shape(COLUMNS, E, dtype=bf16)],
        [own_rows, same, other],
        [acc],
        flops,
    )
    other_tile, sums = call(
        functools.partial(tile_kernel, True),
        [tile, shape(DEPTH, 16, LANES)],
        [other_rows, columns, sums],
        [acc],
        flops,
    )
    sums, other_start = lax.optimization_barrier((sums, other_start))
    sums = exchange(sums, LINE)

    flops = 2 * ROWS * COLUMNS * LANES
    sent = shape(PEERS, HALF + 8, LANES)
    weights = shape(COLUMNS, LANES, dtype=bf16)
    own = shape(HALF, LANES)
    spread = pltpu.VMEM((COLUMNS, LANES), f32)
    mine, packed, inv, root = call(
        first_kernel,
        [sent, weights, own, own],
        [other_tile, sums, start, other_start],
        [spread, spread],
        flops,
    )
    theirs = flip(mine, "core", 1)
    (mine,) = call(again_kernel, [sent], [own_tile, packed, mine], (), flops)
    (total,) = call(narrow_kernel, [shape(PEERS, HALF + 16, LANES, dtype=bf16)], [mine, theirs])
    got = exchange(total, PLANE)
    total, terms = call(
        middle_kernel,
        [shape(DEPTH, HALF + 16, LANES, dtype=bf16), shape(8, LANES)],
        [got, inv, root],
    )
    got = exchange(total, LINE)
    mine, packed = call(second_kernel, [sent, weights], [other_tile, got], (), flops)
    theirs = flip(mine, "core", 1)
    (mine,) = call(again_kernel, [sent], [own_tile, packed, mine], (), flops)
    (total,) = call(add_kernel, [sent], [mine, theirs])
    got = exchange(total, PLANE)
    gram = shape(PEERS, K // 2, LANES)
    vectors, total = call(gram_kernel, [own, gram], [got, inv, root, terms])
    (total,) = call(fold_kernel, [gram], [exchange(total, (*LINE, "core"))])
    got = exchange(total, PLANE)
    (spectral,) = call(
        functools.partial(solve_kernel, math.sqrt(all_docs)), [shape(K, DOCS)], [got, vectors]
    )
    return spectral.T


def solution(mesh):
    fine = Mesh(mesh.devices.reshape(*SIZES.values()), AXES)
    return jax.shard_map(
        local,
        mesh=fine,
        in_specs=(P(AXES, None), P(AXES, None)),
        out_specs=P(AXES, None),
        check_vma=False,
    )
```

```python
import functools
import math

import jax
import jax.numpy as jnp
from jax import lax
from jax.experimental import pallas as pl
from jax.experimental.pallas import tpu as pltpu
from jax.sharding import Mesh
from jax.sharding import PartitionSpec as P

sharpness = 16.0
threshold = 0.3

AXES = ("z", "x", "y", "core")
PLANE = ("x", "y")
LINE = ("z",)
SIZES = {"z": 8, "x": 4, "y": 4, "core": 2}
DEPTH = SIZES["z"]
PEERS = SIZES["x"] * SIZES["y"]

DOCS = 192
HALF = DOCS // 2
E = 256
K = 64
COLUMNS = DEPTH * DOCS
ROWS = PEERS * DOCS
ROW_BLOCK = 3072
COLUMN_BLOCK = 256
LANES = 128
PIVOTS = 8

bf16 = jnp.bfloat16
f32 = jnp.float32
HIGHEST = lax.Precision.HIGHEST


def shape(*dims, dtype=f32):
    return jax.ShapeDtypeStruct(dims, dtype)


def call(kernel, outs, args, scratch=(), flops=0):
    vmem = pl.BlockSpec(memory_space=pltpu.VMEM)
    moved = sum(math.prod(a.shape) * a.dtype.itemsize for a in (*args, *outs))
    return pl.pallas_call(
        kernel,
        out_shape=tuple(outs),
        in_specs=[vmem] * len(args),
        out_specs=tuple(vmem for _ in outs),
        scratch_shapes=list(scratch),
        cost_estimate=pl.CostEstimate(flops=flops, bytes_accessed=moved, transcendentals=0),
        compiler_params=pltpu.CompilerParams(vmem_limit_bytes=8 * 2**20),
    )(*args)


def left_lanes(value):
    return lax.broadcasted_iota(jnp.int32, value.shape, value.ndim - 1) < K


def swap_lanes(value):
    return pltpu.roll(value, K, value.ndim - 1)


def root_of(value):
    guess = lax.rsqrt(value)
    inv = guess * (1.5 - 0.5 * value * guess * guess)
    return inv, value * inv


def two_parts(value):
    hi = value.astype(bf16).astype(f32)
    return hi, (value - hi).astype(bf16).astype(f32)


def unit_kernel(emb_ref, start_ref, line_ref):
    wide = emb_ref[...].astype(f32)
    unit = wide * lax.rsqrt(jnp.sum(wide * wide, axis=1, keepdims=True) + 1e-06)
    line_ref[:, :E] = unit.astype(bf16)
    start = jnp.concatenate([start_ref[...], jnp.zeros((K, 2 * LANES - DOCS), f32)], axis=1)
    start = jnp.concatenate([start, jnp.zeros_like(start)], axis=0).T[:DOCS]
    hi, mid = two_parts(start)
    line_ref[:, E:] = jnp.where(left_lanes(hi), hi, swap_lanes(mid)).astype(bf16)


def plane_kernel(line_ref, plane_ref):
    unit = line_ref[:, :E] * (sharpness / 2)
    plane_ref[...] = jnp.broadcast_to(unit[None], plane_ref.shape)


def tile_kernel(last, *refs):
    if last:
        rows_ref, cols_ref, before_ref, tile_ref, sums_ref, acc = refs
        acc[...] = before_ref[...]
    else:
        rows_ref, *pieces, tile_ref, sums_ref, cols_ref, acc = refs
        acc[...] = jnp.zeros_like(acc)
        for i, piece in enumerate(pieces):
            first = (lax.axis_index("z") + i) % DEPTH * DOCS
            cols_ref[pl.ds(pl.multiple_of(first, DOCS), DOCS), :] = piece[...]

    def block(i, _):
        at = pl.ds(pl.multiple_of(i * ROW_BLOCK, ROW_BLOCK), ROW_BLOCK)
        rows = rows_ref[at, :]
        for c in range(COLUMNS // COLUMN_BLOCK):
            where = slice(c * COLUMN_BLOCK, (c + 1) * COLUMN_BLOCK)
            scores = lax.dot_general(
                rows, cols_ref[where, :E], (((1,), (1,)), ((), ())), preferred_element_type=f32
            )
            entry = jnp.tanh(scores - sharpness * threshold / 2) + 1.0
            tile_ref[at, where] = entry.astype(bf16)
            acc[:, where] += jnp.sum(entry.reshape(ROW_BLOCK // 8, 8, COLUMN_BLOCK), axis=0)
        return 0

    lax.fori_loop(0, ROWS // ROW_BLOCK, block, 0)
    if last:
        total = 0.5 * jnp.sum(acc[...], axis=0, keepdims=True)
        sums_ref[...] = jnp.zeros_like(sums_ref)
        for k in range(COLUMNS // LANES):
            sums_ref[:, k : k + 1, :] = jnp.broadcast_to(
                total[None, :, k * LANES : (k + 1) * LANES], (DEPTH, 1, LANES)
            )
    else:
        sums_ref[...] = acc[...]


def multiply(tile_ref, weights_ref, out_ref, terms):
    chunks = 16

    def block(i, _):
        rows = chunks * DOCS
        sums = jnp.dot(
            tile_ref[pl.ds(pl.multiple_of(i * rows, rows), rows), :],
            weights_ref[...],
            preferred_element_type=f32,
        )
        for c in range(chunks):
            top = sums[c * DOCS : c * DOCS + HALF]
            low = sums[c * DOCS + HALF : (c + 1) * DOCS]
            out_ref[i * chunks + c, :HALF, :] = jnp.where(left_lanes(top), top, low)
            out_ref[i * chunks + c, HALF:, :] = terms
        return 0

    lax.fori_loop(0, PEERS // chunks, block, 0)


def rows_of(*values):
    index = lax.broadcasted_iota(jnp.int32, (8, LANES), 0)
    block = jnp.zeros((8, LANES), f32)
    for i, value in enumerate(values):
        block = jnp.where(index == i, jnp.broadcast_to(value, (8, LANES)), block)
    return block


def spread_lanes(packed):
    other = swap_lanes(packed)
    left = left_lanes(packed)
    return jnp.where(left, packed, other), jnp.where(left, other, packed)


def first_kernel(
    tile_ref, sums_ref, cols_ref, out_ref, weights_ref, inv_ref, root_ref, all_inv, all_root
):
    degree = jnp.sum(sums_ref[...], axis=0)
    blocks = COLUMNS // LANES
    degree = jnp.where(lax.broadcasted_iota(jnp.int32, degree.shape, 0) < blocks, degree, 1.0)
    tall = jnp.concatenate([degree, jnp.ones((LANES - degree.shape[0], LANES), f32)], axis=0).T
    inv, root = root_of(tall)
    correlation = jnp.zeros((1, LANES), f32)
    total = jnp.zeros((1, LANES), f32)
    for k in range(blocks):
        at = slice(k * LANES, (k + 1) * LANES)
        pair = cols_ref[at, E:].astype(f32)
        start = pair + swap_lanes(pair)
        own_inv = jnp.broadcast_to(inv[:, k : k + 1], (LANES, LANES))
        own_root = jnp.broadcast_to(root[:, k : k + 1], (LANES, LANES))
        all_inv[at, :] = own_inv
        all_root[at, :] = own_root
        weights_ref[at, :] = (0.5 * own_inv * start).astype(bf16)
        correlation += jnp.sum(own_root * start, axis=0, keepdims=True)
        total += jnp.sum(
            jnp.broadcast_to(tall[:, k : k + 1], (LANES, LANES)), axis=0, keepdims=True
        )
    first = lax.axis_index("z") * DOCS
    top = pl.ds(pl.multiple_of(first, HALF), HALF)
    low = pl.ds(pl.multiple_of(first + HALF, HALF), HALF)
    for whole, own in ((all_inv, inv_ref), (all_root, root_ref)):
        upper = whole[top, :]
        own[...] = jnp.where(left_lanes(upper), upper, whole[low, :])
    multiply(tile_ref, weights_ref, out_ref, rows_of(correlation, total))


def second_kernel(tile_ref, got_ref, out_ref, weights_ref):
    terms = jnp.zeros((1, LANES), f32)
    for j in range(DEPTH):
        for h, weights in enumerate(spread_lanes(got_ref[j, :HALF, :].astype(f32))):
            at = slice(j * DOCS + h * HALF, j * DOCS + (h + 1) * HALF)
            weights_ref[at, :] = weights.astype(bf16)
        terms += jnp.sum(got_ref[j, HALF:, :].astype(f32), axis=0, keepdims=True)
    multiply(tile_ref, weights_ref, out_ref, rows_of(terms))


def again_kernel(tile_ref, weights_ref, other_ref, out_ref):
    multiply(tile_ref, weights_ref, out_ref, other_ref[0, HALF:, :])


def narrow_kernel(own_ref, other_ref, out_ref):
    out_ref[:, :HALF, :] = (own_ref[:, :HALF, :] + other_ref[:, :HALF, :]).astype(bf16)
    hi, mid = two_parts(own_ref[0, HALF:, :] + other_ref[0, HALF:, :])
    terms = jnp.concatenate([hi, mid], axis=0).astype(bf16)
    out_ref[:, HALF:, :] = jnp.broadcast_to(terms[None], (PEERS, 16, LANES))


def add_kernel(own_ref, other_ref, out_ref):
    out_ref[...] = own_ref[...] + other_ref[...]


def middle_kernel(got_ref, inv_ref, root_ref, out_ref, terms_ref):
    sums = jnp.sum(got_ref[:, :HALF, :].astype(f32), axis=0)
    terms = jnp.sum(got_ref[:, HALF:, :].astype(f32), axis=0)
    terms = terms[:8] + terms[8:]
    terms_ref[...] = terms
    inv, root = inv_ref[...], root_ref[...]
    vectors = inv * sums - root * (terms[0:1] / terms[1:2])
    out_ref[:, :HALF, :] = jnp.broadcast_to(
        (0.5 * inv * vectors).astype(bf16)[None], (DEPTH, HALF, LANES)
    )
    correlation = jnp.sum(root * vectors, axis=0, keepdims=True)
    hi, mid = two_parts(correlation + swap_lanes(correlation))
    index = lax.broadcasted_iota(jnp.int32, (16, LANES), 0)
    terms = jnp.where(index == 0, hi, jnp.where(index == 1, mid, 0.0)).astype(bf16)
    out_ref[:, HALF:, :] = jnp.broadcast_to(terms[None], (DEPTH, 16, LANES))


def gram_kernel(got_ref, inv_ref, root_ref, terms_ref, vectors_ref, out_ref):
    sums = jnp.sum(got_ref[...], axis=0)
    ratio = sums[HALF : HALF + 1] / terms_ref[1:2, :]
    vectors = inv_ref[...] * sums[:HALF] - root_ref[...] * ratio
    vectors_ref[...] = vectors
    tall = jnp.concatenate([vectors, jnp.zeros((LANES - HALF, LANES), f32)], axis=0)
    product = jnp.dot(tall.T, tall, precision=HIGHEST, preferred_element_type=f32)
    gram = product[:K] + swap_lanes(product[K:])
    low = swap_lanes(gram[K // 2 :])
    gram = jnp.where(left_lanes(low), gram[: K // 2], low)
    out_ref[...] = jnp.broadcast_to(gram[None], out_ref.shape)


def fold_kernel(got_ref, out_ref):
    out_ref[...] = jnp.broadcast_to(jnp.sum(got_ref[...], axis=0)[None], out_ref.shape)


def solve_kernel(scale, got_ref, vectors_ref, out_ref):
    packed = jnp.sum(got_ref[...], axis=0)
    work = jnp.concatenate([packed, swap_lanes(packed)], axis=0)
    row = lax.broadcasted_iota(jnp.int32, (K, LANES), 0)
    lane = lax.broadcasted_iota(jnp.int32, (K, LANES), 1)
    work = jnp.where(lane < K, work, jnp.where(lane - K == row, 1.0, 0.0))
    tiles = [work[8 * t : 8 * t + 8] for t in range(K // 8)]
    index = lax.broadcasted_iota(jnp.int32, (8, LANES), 0)
    for k in range(0, K, PIVOTS):
        first, place = divmod(k, 8)
        rows = [tiles[first][place + i : place + i + 1] for i in range(PIVOTS)]
        inner = {
            (i, j): jnp.broadcast_to(rows[i][:, k + j : k + j + 1], (1, LANES))
            for i in range(PIVOTS)
            for j in range(i, PIVOTS)
        }
        after = range(first, K // 8)
        columns = [
            {t: jnp.broadcast_to(tiles[t][:, k + i : k + i + 1], (8, LANES)) for t in after}
            for i in range(PIVOTS)
        ]
        for i in range(PIVOTS):
            inverse = 1.0 / inner[i, i]
            for m in range(i + 1, PIVOTS):
                factor = inner[i, m] * inverse
                rows[m] = rows[m] - factor * rows[i]
                for j in range(m, PIVOTS):
                    inner[m, j] = inner[m, j] - factor * inner[i, j]
                for t in after:
                    columns[m][t] = columns[m][t] - columns[i][t] * factor
            pivot_row = rows[i] * inverse
            for t in after:
                column = columns[i][t]
                if t == first:
                    column = jnp.where(index > place + i, column, 0.0)
                tiles[t] = tiles[t] - column * pivot_row
    work = jnp.concatenate(tiles, axis=0)
    pivots = jnp.sum(jnp.where(lane == row, work, 0.0), axis=1, keepdims=True)
    inv, _ = root_of(pivots)
    right = jnp.where(lane < K, 0.0, work * (inv * scale))
    low = vectors_ref[...]
    padding = jnp.zeros((2 * LANES - DOCS, LANES), f32)
    vectors = jnp.concatenate([swap_lanes(low), low, padding], axis=0)
    out_ref[...] = lax.dot_general(
        right, vectors, (((1,), (1,)), ((), ())), precision=HIGHEST, preferred_element_type=f32
    )[:, :DOCS]


def exchange(value, axes):
    return lax.all_to_all(value, axes, 0, 0, tiled=True)


def swap_core(value):
    return lax.ppermute(value, "core", [(0, 1), (1, 0)])


def shift(value, step):
    return lax.ppermute(value, "z", [(i, (i + step) % DEPTH) for i in range(DEPTH)])


def local(embeddings, start_vectors):
    all_docs = embeddings.shape[0] * lax.axis_size(AXES)
    width = E + 2 * K
    (line,) = call(
        unit_kernel, [shape(DOCS, width, dtype=bf16)], [embeddings, start_vectors.T]
    )
    (plane,) = call(plane_kernel, [shape(PEERS, DOCS, E, dtype=bf16)], [line])
    pieces = [line] + [None] * (DEPTH - 1)
    behind = ahead = line
    for i in range(1, DEPTH // 2):
        behind, ahead = shift(behind, 1), shift(ahead, -1)
        pieces[-i], pieces[i] = behind, ahead
    pieces[DEPTH // 2] = shift(ahead, -1)
    own_rows, *pieces = lax.optimization_barrier((exchange(plane, PLANE), *pieces))
    own_rows = own_rows.reshape(ROWS, E)
    other_rows = swap_core(own_rows)

    tile = shape(ROWS, COLUMNS, dtype=bf16)
    acc = pltpu.VMEM((8, COLUMNS), f32)
    flops = 2 * ROWS * COLUMNS * E
    own_tile, sums, columns = call(
        functools.partial(tile_kernel, False),
        [tile, shape(8, COLUMNS), shape(COLUMNS, width, dtype=bf16)],
        [own_rows, *pieces],
        [acc],
        flops,
    )
    other_tile, sums = call(
        functools.partial(tile_kernel, True),
        [tile, shape(DEPTH, 16, LANES)],
        [other_rows, columns, sums],
        [acc],
        flops,
    )
    sums = exchange(sums, LINE)

    flops = 2 * ROWS * COLUMNS * LANES
    sent = shape(PEERS, HALF + 8, LANES)
    weights = shape(COLUMNS, LANES, dtype=bf16)
    own = shape(HALF, LANES)
    spread = pltpu.VMEM((COLUMNS, LANES), f32)
    mine, packed, inv, root = call(
        first_kernel,
        [sent, weights, own, own],
        [other_tile, sums, columns],
        [spread, spread],
        flops,
    )
    theirs = swap_core(mine)
    (mine,) = call(again_kernel, [sent], [own_tile, packed, mine], (), flops)
    (total,) = call(narrow_kernel, [shape(PEERS, HALF + 16, LANES, dtype=bf16)], [mine, theirs])
    got = exchange(total, PLANE)
    total, terms = call(
        middle_kernel,
        [shape(DEPTH, HALF + 16, LANES, dtype=bf16), shape(8, LANES)],
        [got, inv, root],
    )
    got = exchange(total, LINE)
    mine, packed = call(second_kernel, [sent, weights], [other_tile, got], (), flops)
    theirs = swap_core(mine)
    (mine,) = call(again_kernel, [sent], [own_tile, packed, mine], (), flops)
    (total,) = call(add_kernel, [sent], [mine, theirs])
    got = exchange(total, PLANE)
    gram = shape(PEERS, K // 2, LANES)
    vectors, total = call(gram_kernel, [own, gram], [got, inv, root, terms])
    (total,) = call(fold_kernel, [gram], [exchange(total, (*LINE, "core"))])
    got = exchange(total, PLANE)
    (spectral,) = call(
        functools.partial(solve_kernel, math.sqrt(all_docs)), [shape(K, DOCS)], [got, vectors]
    )
    return spectral.T


def solution(mesh):
    fine = Mesh(mesh.devices.reshape(*SIZES.values()), AXES)
    return jax.shard_map(
        local,
        mesh=fine,
        in_specs=(P(AXES, None), P(AXES, None)),
        out_specs=P(AXES, None),
        check_vma=False,
    )
```

```python
import functools
import math

import jax
import jax.numpy as jnp
from jax import lax
from jax.experimental import pallas as pl
from jax.experimental.pallas import tpu as pltpu
from jax.sharding import Mesh
from jax.sharding import PartitionSpec as P

sharpness = 16.0
threshold = 0.3

AXES = ("z", "x", "y", "core")
PLANE = ("x", "y")
LINE = ("z",)
SIZES = {"z": 8, "x": 4, "y": 4, "core": 2}
DEPTH = SIZES["z"]
PEERS = SIZES["x"] * SIZES["y"]

DOCS = 192
HALF = DOCS // 2
E = 256
K = 64
COLUMNS = DEPTH * DOCS
ROWS = PEERS * DOCS
ROW_BLOCK = 3072
COLUMN_BLOCK = 256
LANES = 128
PIVOTS = 8
PACKED = 24
MERGE_COST = 10_350_000_000

bf16 = jnp.bfloat16
f32 = jnp.float32
HIGHEST = lax.Precision.HIGHEST


def shape(*dims, dtype=f32):
    return jax.ShapeDtypeStruct(dims, dtype)


def call(kernel, outs, args, scratch=(), flops=0, space=pltpu.VMEM):
    vmem = pl.BlockSpec(memory_space=pltpu.VMEM)
    moved = sum(math.prod(a.shape) * a.dtype.itemsize for a in (*args, *outs))
    return pl.pallas_call(
        kernel,
        out_shape=tuple(outs),
        in_specs=[pl.BlockSpec(memory_space=space)] * len(args),
        out_specs=tuple(vmem for _ in outs),
        scratch_shapes=list(scratch),
        cost_estimate=pl.CostEstimate(flops=flops, bytes_accessed=moved, transcendentals=0),
        compiler_params=pltpu.CompilerParams(vmem_limit_bytes=8 * 2**20),
    )(*args)


def left_lanes(value):
    return lax.broadcasted_iota(jnp.int32, value.shape, value.ndim - 1) < K


def swap_lanes(value):
    return pltpu.roll(value, K, value.ndim - 1)


def root_of(value):
    guess = lax.rsqrt(value)
    inv = guess * (1.5 - 0.5 * value * guess * guess)
    return inv, value * inv


def two_parts(value):
    hi = value.astype(bf16).astype(f32)
    return hi, (value - hi).astype(bf16).astype(f32)


def unit_kernel(emb_hbm, start_hbm, line_ref, emb_ref, start_ref, done):
    copies = [
        pltpu.make_async_copy(emb_hbm, emb_ref, done.at[0]),
        pltpu.make_async_copy(start_hbm, start_ref, done.at[1]),
    ]
    for copy in copies:
        copy.start()
    for copy in copies:
        copy.wait()
    wide = emb_ref[...].astype(f32)
    unit = wide * lax.rsqrt(jnp.sum(wide * wide, axis=1, keepdims=True) + 1e-06)
    line_ref[:, :E] = unit.astype(bf16)
    start = jnp.concatenate([start_ref[...], jnp.zeros((K, 2 * LANES - DOCS), f32)], axis=1)
    start = jnp.concatenate([start, jnp.zeros_like(start)], axis=0).T[:DOCS]
    hi, mid = two_parts(start)
    line_ref[:, E:] = jnp.where(left_lanes(hi), hi, swap_lanes(mid)).astype(bf16)


def plane_kernel(line_ref, plane_ref):
    unit = line_ref[:, :E] * (sharpness / 2)
    plane_ref[...] = jnp.broadcast_to(unit[None], plane_ref.shape)


def merge_kernel(*refs):
    *pieces, cols_ref = refs
    for i, piece in enumerate(pieces):
        first = (lax.axis_index("z") + i) % DEPTH * DOCS
        cols_ref[pl.ds(pl.multiple_of(first, DOCS), DOCS), :] = piece[...]


def tile_kernel(last, *refs):
    if last:
        rows_ref, cols_ref, before_ref, tile_ref, sums_ref, acc = refs
        acc[...] = before_ref[...]
    else:
        rows_ref, cols_ref, tile_ref, sums_ref, acc = refs
        acc[...] = jnp.zeros_like(acc)

    def block(i, _):
        at = pl.ds(pl.multiple_of(i * ROW_BLOCK, ROW_BLOCK), ROW_BLOCK)
        rows = rows_ref[at, :]
        for c in range(COLUMNS // COLUMN_BLOCK):
            where = slice(c * COLUMN_BLOCK, (c + 1) * COLUMN_BLOCK)
            scores = lax.dot_general(
                rows, cols_ref[where, :E], (((1,), (1,)), ((), ())), preferred_element_type=f32
            )
            entry = jnp.tanh(scores - sharpness * threshold / 2) + 1.0
            tile_ref[at, where] = entry.astype(bf16)
            acc[:, where] += jnp.sum(entry.reshape(ROW_BLOCK // 8, 8, COLUMN_BLOCK), axis=0)
        return 0

    lax.fori_loop(0, ROWS // ROW_BLOCK, block, 0)
    if last:
        total = 0.5 * jnp.sum(acc[...], axis=0, keepdims=True)
        sums_ref[...] = jnp.zeros_like(sums_ref)
        for k in range(COLUMNS // LANES):
            sums_ref[:, k : k + 1, :] = jnp.broadcast_to(
                total[None, :, k * LANES : (k + 1) * LANES], (DEPTH, 1, LANES)
            )
    else:
        sums_ref[...] = acc[...]


def multiply(tile_ref, weights_ref, out_ref, terms):
    chunks = 16

    def block(i, _):
        rows = chunks * DOCS
        sums = jnp.dot(
            tile_ref[pl.ds(pl.multiple_of(i * rows, rows), rows), :],
            weights_ref[...],
            preferred_element_type=f32,
        )
        for c in range(chunks):
            top = sums[c * DOCS : c * DOCS + HALF]
            low = sums[c * DOCS + HALF : (c + 1) * DOCS]
            out_ref[i * chunks + c, :HALF, :] = jnp.where(left_lanes(top), top, low)
            out_ref[i * chunks + c, HALF:, :] = terms
        return 0

    lax.fori_loop(0, PEERS // chunks, block, 0)


def rows_of(*values):
    index = lax.broadcasted_iota(jnp.int32, (8, LANES), 0)
    block = jnp.zeros((8, LANES), f32)
    for i, value in enumerate(values):
        block = jnp.where(index == i, jnp.broadcast_to(value, (8, LANES)), block)
    return block


def spread_lanes(packed):
    other = swap_lanes(packed)
    left = left_lanes(packed)
    return jnp.where(left, packed, other), jnp.where(left, other, packed)


def first_kernel(
    tile_ref, sums_ref, cols_ref, out_ref, weights_ref, inv_ref, root_ref, all_inv, all_root
):
    degree = jnp.sum(sums_ref[...], axis=0)
    blocks = COLUMNS // LANES
    degree = jnp.where(lax.broadcasted_iota(jnp.int32, degree.shape, 0) < blocks, degree, 1.0)
    tall = jnp.concatenate([degree, jnp.ones((LANES - degree.shape[0], LANES), f32)], axis=0).T
    inv, root = root_of(tall)
    correlation = jnp.zeros((1, LANES), f32)
    total = jnp.zeros((1, LANES), f32)
    for k in range(blocks):
        at = slice(k * LANES, (k + 1) * LANES)
        pair = cols_ref[at, E:].astype(f32)
        start = pair + swap_lanes(pair)
        own_inv = jnp.broadcast_to(inv[:, k : k + 1], (LANES, LANES))
        own_root = jnp.broadcast_to(root[:, k : k + 1], (LANES, LANES))
        all_inv[at, :] = own_inv
        all_root[at, :] = own_root
        weights_ref[at, :] = (0.5 * own_inv * start).astype(bf16)
        correlation += jnp.sum(own_root * start, axis=0, keepdims=True)
        total += jnp.sum(
            jnp.broadcast_to(tall[:, k : k + 1], (LANES, LANES)), axis=0, keepdims=True
        )
    first = lax.axis_index("z") * DOCS
    top = pl.ds(pl.multiple_of(first, HALF), HALF)
    low = pl.ds(pl.multiple_of(first + HALF, HALF), HALF)
    for whole, own in ((all_inv, inv_ref), (all_root, root_ref)):
        upper = whole[top, :]
        own[...] = jnp.where(left_lanes(upper), upper, whole[low, :])
    multiply(tile_ref, weights_ref, out_ref, rows_of(correlation, total))


def second_kernel(tile_ref, got_ref, out_ref, weights_ref):
    terms = jnp.zeros((1, LANES), f32)
    for j in range(DEPTH):
        for h, weights in enumerate(spread_lanes(got_ref[j, :HALF, :].astype(f32))):
            at = slice(j * DOCS + h * HALF, j * DOCS + (h + 1) * HALF)
            weights_ref[at, :] = weights.astype(bf16)
        terms += jnp.sum(got_ref[j, HALF:, :].astype(f32), axis=0, keepdims=True)
    multiply(tile_ref, weights_ref, out_ref, rows_of(terms))


def again_kernel(tile_ref, weights_ref, other_ref, out_ref):
    multiply(tile_ref, weights_ref, out_ref, other_ref[0, HALF:, :])


def narrow_kernel(own_ref, other_ref, out_ref):
    out_ref[:, :HALF, :] = (own_ref[:, :HALF, :] + other_ref[:, :HALF, :]).astype(bf16)
    hi, mid = two_parts(own_ref[0, HALF:, :] + other_ref[0, HALF:, :])
    terms = jnp.concatenate([hi, mid], axis=0).astype(bf16)
    out_ref[:, HALF:, :] = jnp.broadcast_to(terms[None], (PEERS, 16, LANES))


def add_kernel(own_ref, other_ref, out_ref):
    out_ref[...] = own_ref[...] + other_ref[...]


def middle_kernel(got_ref, inv_ref, root_ref, out_ref, terms_ref):
    sums = jnp.sum(got_ref[:, :HALF, :].astype(f32), axis=0)
    terms = jnp.sum(got_ref[:, HALF:, :].astype(f32), axis=0)
    terms = terms[:8] + terms[8:]
    terms_ref[...] = terms
    inv, root = inv_ref[...], root_ref[...]
    vectors = inv * sums - root * (terms[0:1] / terms[1:2])
    out_ref[:, :HALF, :] = jnp.broadcast_to(
        (0.5 * inv * vectors).astype(bf16)[None], (DEPTH, HALF, LANES)
    )
    correlation = jnp.sum(root * vectors, axis=0, keepdims=True)
    hi, mid = two_parts(correlation + swap_lanes(correlation))
    index = lax.broadcasted_iota(jnp.int32, (16, LANES), 0)
    terms = jnp.where(index == 0, hi, jnp.where(index == 1, mid, 0.0)).astype(bf16)
    out_ref[:, HALF:, :] = jnp.broadcast_to(terms[None], (DEPTH, 16, LANES))


def gram_kernel(got_ref, inv_ref, root_ref, terms_ref, vectors_ref, out_ref):
    sums = jnp.sum(got_ref[...], axis=0)
    ratio = sums[HALF : HALF + 1] / terms_ref[1:2, :]
    vectors = inv_ref[...] * sums[:HALF] - root_ref[...] * ratio
    vectors_ref[...] = vectors
    tall = jnp.concatenate([vectors, jnp.zeros((LANES - HALF, LANES), f32)], axis=0)
    product = jnp.dot(tall.T, tall, precision=HIGHEST, preferred_element_type=f32)
    gram = product[:K] + swap_lanes(product[K:])
    quarter = K // 2
    lane = lax.broadcasted_iota(jnp.int32, (quarter, LANES), 1)
    low = gram[quarter:]
    packed = jnp.where(lane < quarter, gram[:quarter], jnp.where(lane < K, low, swap_lanes(low)))
    tail = packed[PACKED:]
    folded = jnp.concatenate(
        [pltpu.roll(tail, LANES - quarter * (i + 1), 1) for i in range(3)], axis=0
    )
    out_ref[...] = jnp.broadcast_to(
        jnp.where(lane[:PACKED] < 3 * quarter, packed[:PACKED], folded)[None], out_ref.shape
    )


def fold_kernel(got_ref, out_ref):
    out_ref[...] = jnp.broadcast_to(jnp.sum(got_ref[...], axis=0)[None], out_ref.shape)


def solve_kernel(scale, got_ref, vectors_ref, out_ref):
    packed = jnp.sum(got_ref[...], axis=0)
    quarter = K // 2
    piece = lax.broadcasted_iota(jnp.int32, (8, LANES), 1) // quarter
    tail = jnp.zeros((8, LANES), f32)
    for i in range(3):
        tail = jnp.where(piece == i, pltpu.roll(packed[8 * i : 8 * i + 8], quarter * (i + 1), 1), tail)
    packed = jnp.concatenate([packed, tail], axis=0)
    lane = lax.broadcasted_iota(jnp.int32, packed.shape, 1)
    low = jnp.where(lane < quarter, swap_lanes(packed), packed)
    whole = jnp.concatenate([packed, low, jnp.zeros((LANES - K, LANES), f32)], axis=0)
    turned = whole.T
    upper = jnp.where(lane < quarter, packed, turned[:quarter])
    work = jnp.concatenate([upper, low], axis=0)
    row = lax.broadcasted_iota(jnp.int32, (K, LANES), 0)
    lane = lax.broadcasted_iota(jnp.int32, (K, LANES), 1)
    work = jnp.where(lane < K, work, jnp.where(lane - K == row, 1.0, 0.0))
    tiles = [work[8 * t : 8 * t + 8] for t in range(K // 8)]
    index = lax.broadcasted_iota(jnp.int32, (8, LANES), 0)
    for k in range(0, K, PIVOTS):
        first, place = divmod(k, 8)
        rows = [tiles[first][place + i : place + i + 1] for i in range(PIVOTS)]
        inner = {
            (i, j): jnp.broadcast_to(rows[i][:, k + j : k + j + 1], (1, LANES))
            for i in range(PIVOTS)
            for j in range(i, PIVOTS)
        }
        after = range(first, K // 8)
        columns = [
            {t: jnp.broadcast_to(tiles[t][:, k + i : k + i + 1], (8, LANES)) for t in after}
            for i in range(PIVOTS)
        ]
        for i in range(PIVOTS):
            inverse = 1.0 / inner[i, i]
            for m in range(i + 1, PIVOTS):
                factor = inner[i, m] * inverse
                rows[m] = rows[m] - factor * rows[i]
                for j in range(m, PIVOTS):
                    inner[m, j] = inner[m, j] - factor * inner[i, j]
                for t in after:
                    columns[m][t] = columns[m][t] - columns[i][t] * factor
            pivot_row = rows[i] * inverse
            for t in after:
                column = columns[i][t]
                if t == first:
                    column = jnp.where(index > place + i, column, 0.0)
                tiles[t] = tiles[t] - column * pivot_row
    work = jnp.concatenate(tiles, axis=0)
    pivots = jnp.sum(jnp.where(lane == row, work, 0.0), axis=1, keepdims=True)
    inv, _ = root_of(pivots)
    right = jnp.where(lane < K, 0.0, work * (inv * scale))
    low = vectors_ref[...]
    padding = jnp.zeros((2 * LANES - DOCS, LANES), f32)
    vectors = jnp.concatenate([swap_lanes(low), low, padding], axis=0)
    out_ref[...] = lax.dot_general(
        right, vectors, (((1,), (1,)), ((), ())), precision=HIGHEST, preferred_element_type=f32
    )[:, :DOCS]


def exchange(value, axes):
    return lax.all_to_all(value, axes, 0, 0, tiled=True)


def swap_core(value):
    return lax.ppermute(value, "core", [(0, 1), (1, 0)])


def shift(value, step):
    return lax.ppermute(value, "z", [(i, (i + step) % DEPTH) for i in range(DEPTH)])


def local(embeddings, start_vectors):
    all_docs = embeddings.shape[0] * lax.axis_size(AXES)
    width = E + 2 * K
    (line,) = call(
        unit_kernel,
        [shape(DOCS, width, dtype=bf16)],
        [
            pltpu.with_memory_space_constraint(value, pltpu.HBM)
            for value in (embeddings, start_vectors.T)
        ],
        [
            pltpu.VMEM((DOCS, E), bf16),
            pltpu.VMEM((K, DOCS), f32),
            pltpu.SemaphoreType.DMA((2,)),
        ],
        space=pltpu.HBM,
    )
    (plane,) = call(plane_kernel, [shape(PEERS, DOCS, E, dtype=bf16)], [line])
    pieces = [line] + [None] * (DEPTH - 1)
    behind = ahead = line
    for i in range(1, DEPTH // 2):
        behind, ahead = shift(behind, 1), shift(ahead, -1)
        pieces[-i], pieces[i] = behind, ahead
    pieces[DEPTH // 2] = shift(ahead, -1)
    (columns,) = call(
        merge_kernel, [shape(COLUMNS, width, dtype=bf16)], pieces, (), MERGE_COST
    )
    own_rows, columns = lax.optimization_barrier((exchange(plane, PLANE), columns))
    own_rows = own_rows.reshape(ROWS, E)
    other_rows = swap_core(own_rows)

    tile = shape(ROWS, COLUMNS, dtype=bf16)
    acc = pltpu.VMEM((8, COLUMNS), f32)
    flops = 2 * ROWS * COLUMNS * E
    own_tile, sums = call(
        functools.partial(tile_kernel, False),
        [tile, shape(8, COLUMNS)],
        [own_rows, columns],
        [acc],
        flops,
    )
    other_tile, sums = call(
        functools.partial(tile_kernel, True),
        [tile, shape(DEPTH, 16, LANES)],
        [other_rows, columns, sums],
        [acc],
        flops,
    )
    sums = exchange(sums, LINE)

    flops = 2 * ROWS * COLUMNS * LANES
    sent = shape(PEERS, HALF + 8, LANES)
    weights = shape(COLUMNS, LANES, dtype=bf16)
    own = shape(HALF, LANES)
    spread = pltpu.VMEM((COLUMNS, LANES), f32)
    mine, packed, inv, root = call(
        first_kernel,
        [sent, weights, own, own],
        [other_tile, sums, columns],
        [spread, spread],
        flops,
    )
    theirs = swap_core(mine)
    (mine,) = call(again_kernel, [sent], [own_tile, packed, mine], (), flops)
    (total,) = call(narrow_kernel, [shape(PEERS, HALF + 16, LANES, dtype=bf16)], [mine, theirs])
    got = exchange(total, PLANE)
    total, terms = call(
        middle_kernel,
        [shape(DEPTH, HALF + 16, LANES, dtype=bf16), shape(8, LANES)],
        [got, inv, root],
    )
    got = exchange(total, LINE)
    mine, packed = call(second_kernel, [sent, weights], [other_tile, got], (), flops)
    theirs = swap_core(mine)
    (mine,) = call(again_kernel, [sent], [own_tile, packed, mine], (), flops)
    (total,) = call(add_kernel, [sent], [mine, theirs])
    got = exchange(total, PLANE)
    gram = shape(PEERS, PACKED, LANES)
    vectors, total = call(gram_kernel, [own, gram], [got, inv, root, terms])
    (total,) = call(fold_kernel, [gram], [exchange(total, (*LINE, "core"))])
    got = exchange(total, PLANE)
    (spectral,) = call(
        functools.partial(solve_kernel, math.sqrt(all_docs)), [shape(K, DOCS)], [got, vectors]
    )
    return spectral.T


def solution(mesh):
    fine = Mesh(mesh.devices.reshape(*SIZES.values()), AXES)
    return jax.shard_map(
        local,
        mesh=fine,
        in_specs=(P(AXES, None), P(AXES, None)),
        out_specs=P(AXES, None),
        check_vma=False,
    )
```

```python
import functools
import math

import jax
import jax.numpy as jnp
from jax import lax
from jax.experimental import pallas as pl
from jax.experimental.pallas import tpu as pltpu
from jax.sharding import Mesh
from jax.sharding import PartitionSpec as P

sharpness = 16.0
threshold = 0.3

AXES = ("z", "x", "y", "core")
PLANE = ("x", "y")
LINE = ("z",)
SIZES = {"z": 8, "x": 4, "y": 4, "core": 2}
DEPTH = SIZES["z"]
PEERS = SIZES["x"] * SIZES["y"]

DOCS = 192
HALF = DOCS // 2
E = 256
K = 64
COLUMNS = DEPTH * DOCS
ROWS = PEERS * DOCS
ROW_BLOCK = 3072
COLUMN_BLOCK = 256
LANES = 128
PIVOTS = 8
SAMPLE = 24
PACKED = 24
MERGE_COST = 10_350_000_000

bf16 = jnp.bfloat16
f32 = jnp.float32
HIGHEST = lax.Precision.HIGHEST


def shape(*dims, dtype=f32):
    return jax.ShapeDtypeStruct(dims, dtype)


def call(kernel, outs, args, scratch=(), flops=0, space=pltpu.VMEM):
    vmem = pl.BlockSpec(memory_space=pltpu.VMEM)
    moved = sum(math.prod(a.shape) * a.dtype.itemsize for a in (*args, *outs))
    return pl.pallas_call(
        kernel,
        out_shape=tuple(outs),
        in_specs=[pl.BlockSpec(memory_space=space)] * len(args),
        out_specs=tuple(vmem for _ in outs),
        scratch_shapes=list(scratch),
        cost_estimate=pl.CostEstimate(flops=flops, bytes_accessed=moved, transcendentals=0),
        compiler_params=pltpu.CompilerParams(vmem_limit_bytes=8 * 2**20),
    )(*args)


def left_lanes(value):
    return lax.broadcasted_iota(jnp.int32, value.shape, value.ndim - 1) < K


def swap_lanes(value):
    return pltpu.roll(value, K, value.ndim - 1)


def root_of(value):
    guess = lax.rsqrt(value)
    inv = guess * (1.5 - 0.5 * value * guess * guess)
    return inv, value * inv


def two_parts(value):
    hi = value.astype(bf16).astype(f32)
    return hi, (value - hi).astype(bf16).astype(f32)


def unit_kernel(emb_hbm, start_hbm, line_ref, emb_ref, start_ref, done):
    copies = [
        pltpu.make_async_copy(emb_hbm, emb_ref, done.at[0]),
        pltpu.make_async_copy(start_hbm, start_ref, done.at[1]),
    ]
    for copy in copies:
        copy.start()
    for copy in copies:
        copy.wait()
    wide = emb_ref[...].astype(f32)
    unit = wide * lax.rsqrt(jnp.sum(wide * wide, axis=1, keepdims=True) + 1e-06)
    line_ref[:, :E] = unit.astype(bf16)
    start = jnp.concatenate([start_ref[...], jnp.zeros((K, 2 * LANES - DOCS), f32)], axis=1)
    start = jnp.concatenate([start, jnp.zeros_like(start)], axis=0).T[:DOCS]
    hi, mid = two_parts(start)
    line_ref[:, E:] = jnp.where(left_lanes(hi), hi, swap_lanes(mid)).astype(bf16)


def plane_kernel(line_ref, plane_ref):
    unit = line_ref[:, :E] * (sharpness / 2)
    plane_ref[...] = jnp.broadcast_to(unit[None], plane_ref.shape)


def merge_kernel(*refs):
    *pieces, cols_ref = refs
    for i, piece in enumerate(pieces):
        first = (lax.axis_index("z") + i) % DEPTH * DOCS
        cols_ref[pl.ds(pl.multiple_of(first, DOCS), DOCS), :] = piece[...]


def tile_kernel(last, *refs):
    if last:
        rows_ref, cols_ref, before_ref, tile_ref, sums_ref, acc = refs
        acc[...] = before_ref[...]
    else:
        rows_ref, cols_ref, tile_ref, sums_ref, acc = refs
        acc[...] = jnp.zeros_like(acc)

    def block(i, _):
        at = pl.ds(pl.multiple_of(i * ROW_BLOCK, ROW_BLOCK), ROW_BLOCK)
        rows = rows_ref[at, :]
        for c in range(COLUMNS // COLUMN_BLOCK):
            where = slice(c * COLUMN_BLOCK, (c + 1) * COLUMN_BLOCK)
            scores = lax.dot_general(
                rows, cols_ref[where, :E], (((1,), (1,)), ((), ())), preferred_element_type=f32
            )
            entry = jnp.tanh(scores - sharpness * threshold / 2) + 1.0
            tile_ref[at, where] = entry.astype(bf16)
            acc[:, where] += jnp.sum(entry.reshape(ROW_BLOCK // 8, 8, COLUMN_BLOCK), axis=0)
        return 0

    lax.fori_loop(0, ROWS // ROW_BLOCK, block, 0)
    if last:
        total = 0.5 * jnp.sum(acc[...], axis=0, keepdims=True)
        sums_ref[...] = jnp.zeros_like(sums_ref)
        for k in range(COLUMNS // LANES):
            sums_ref[:, k : k + 1, :] = jnp.broadcast_to(
                total[None, :, k * LANES : (k + 1) * LANES], (DEPTH, 1, LANES)
            )
    else:
        sums_ref[...] = acc[...]


def multiply(tile_ref, weights_ref, out_ref, terms):
    chunks = 16

    def block(i, _):
        rows = chunks * DOCS
        sums = jnp.dot(
            tile_ref[pl.ds(pl.multiple_of(i * rows, rows), rows), :],
            weights_ref[...],
            preferred_element_type=f32,
        )
        for c in range(chunks):
            top = sums[c * DOCS : c * DOCS + HALF]
            low = sums[c * DOCS + HALF : (c + 1) * DOCS]
            out_ref[i * chunks + c, :HALF, :] = jnp.where(left_lanes(top), top, low)
            out_ref[i * chunks + c, HALF:, :] = terms
        return 0

    lax.fori_loop(0, PEERS // chunks, block, 0)


def rows_of(*values):
    index = lax.broadcasted_iota(jnp.int32, (8, LANES), 0)
    block = jnp.zeros((8, LANES), f32)
    for i, value in enumerate(values):
        block = jnp.where(index == i, jnp.broadcast_to(value, (8, LANES)), block)
    return block


def spread_lanes(packed):
    other = swap_lanes(packed)
    left = left_lanes(packed)
    return jnp.where(left, packed, other), jnp.where(left, other, packed)


def first_kernel(
    tile_ref, sums_ref, cols_ref, out_ref, weights_ref, inv_ref, root_ref, all_inv, all_root
):
    degree = jnp.sum(sums_ref[...], axis=0)
    blocks = COLUMNS // LANES
    degree = jnp.where(lax.broadcasted_iota(jnp.int32, degree.shape, 0) < blocks, degree, 1.0)
    tall = jnp.concatenate([degree, jnp.ones((LANES - degree.shape[0], LANES), f32)], axis=0).T
    inv, root = root_of(tall)
    correlation = jnp.zeros((1, LANES), f32)
    total = jnp.zeros((1, LANES), f32)
    for k in range(blocks):
        at = slice(k * LANES, (k + 1) * LANES)
        pair = cols_ref[at, E:].astype(f32)
        start = pair + swap_lanes(pair)
        own_inv = jnp.broadcast_to(inv[:, k : k + 1], (LANES, LANES))
        own_root = jnp.broadcast_to(root[:, k : k + 1], (LANES, LANES))
        all_inv[at, :] = own_inv
        all_root[at, :] = own_root
        weights_ref[at, :] = (0.5 * own_inv * start).astype(bf16)
        correlation += jnp.sum(own_root * start, axis=0, keepdims=True)
        total += jnp.sum(
            jnp.broadcast_to(tall[:, k : k + 1], (LANES, LANES)), axis=0, keepdims=True
        )
    first = lax.axis_index("z") * DOCS
    top = pl.ds(pl.multiple_of(first, HALF), HALF)
    low = pl.ds(pl.multiple_of(first + HALF, HALF), HALF)
    for whole, own in ((all_inv, inv_ref), (all_root, root_ref)):
        upper = whole[top, :]
        own[...] = jnp.where(left_lanes(upper), upper, whole[low, :])
    multiply(tile_ref, weights_ref, out_ref, rows_of(correlation, total))


def second_kernel(tile_ref, got_ref, out_ref, weights_ref):
    terms = jnp.zeros((1, LANES), f32)
    for j in range(DEPTH):
        for h, weights in enumerate(spread_lanes(got_ref[j, :HALF, :].astype(f32))):
            at = slice(j * DOCS + h * HALF, j * DOCS + (h + 1) * HALF)
            weights_ref[at, :] = weights.astype(bf16)
        terms += jnp.sum(got_ref[j, HALF:, :].astype(f32), axis=0, keepdims=True)
    multiply(tile_ref, weights_ref, out_ref, rows_of(terms))


def again_kernel(tile_ref, weights_ref, other_ref, out_ref):
    multiply(tile_ref, weights_ref, out_ref, other_ref[0, HALF:, :])


def narrow_kernel(own_ref, other_ref, out_ref):
    out_ref[:, :HALF, :] = (own_ref[:, :HALF, :] + other_ref[:, :HALF, :]).astype(bf16)
    hi, mid = two_parts(own_ref[0, HALF:, :] + other_ref[0, HALF:, :])
    terms = jnp.concatenate([hi, mid], axis=0).astype(bf16)
    out_ref[:, HALF:, :] = jnp.broadcast_to(terms[None], (PEERS, 16, LANES))


def split_kernel(own_ref, other_ref, out_ref):
    sums = own_ref[:, :HALF, :] + other_ref[:, :HALF, :]
    sample = sums[:, :SAMPLE].reshape(PEERS * SAMPLE, LANES)
    gram = lax.dot_general(sample, sample, (((0,), (0,)), ((), ())), preferred_element_type=f32)
    gram = gram[:K] + swap_lanes(gram[K:])
    gram = jnp.concatenate([jnp.where(left_lanes(gram), gram, 0.0), jnp.zeros_like(gram)], axis=0)
    main = jnp.dot(gram[:8], gram, preferred_element_type=f32)[:1]
    main = main * lax.rsqrt(jnp.sum(main * main) + 1e-30)
    main = main.astype(bf16).astype(f32)
    both = main + swap_lanes(main)
    row = lax.broadcasted_iota(jnp.int32, (LANES, LANES), 0)
    turned = jnp.where((row < K) == left_lanes(row), both, 0.0).astype(bf16)
    wide = jnp.concatenate([sums, jnp.zeros((PEERS, LANES - HALF, LANES), f32)], axis=1)
    wide = wide.reshape(PEERS * LANES, LANES).astype(bf16)
    factor = lax.dot_general(
        wide, turned, (((1,), (1,)), ((), ())), preferred_element_type=f32
    ).astype(bf16)
    known = (factor.astype(f32) * both).reshape(PEERS, LANES, LANES)
    out_ref[:, :HALF, :] = (sums - known[:, :HALF]).astype(bf16)
    index = lax.broadcasted_iota(jnp.int32, (8, LANES), 0)
    lane = lax.broadcasted_iota(jnp.int32, (8, LANES), 1)
    pick = jnp.where((lane == index * K) & (index < 2), 1.0, 0.0).astype(bf16)
    rows = lax.dot_general(pick, factor, (((1,), (1,)), ((), ())), preferred_element_type=f32)
    hi, mid = two_parts(own_ref[0, HALF : HALF + 1, :] + other_ref[0, HALF : HALF + 1, :])
    low = jnp.where(index == 0, main, jnp.where(index == 1, swap_lanes(main), 0.0))
    low = jnp.where(index == 2, hi, jnp.where(index == 3, mid, low))
    for p in range(PEERS):
        top = rows[:, p * LANES : (p + 1) * LANES]
        out_ref[p, HALF:, :] = jnp.concatenate([top, low], axis=0).astype(bf16)


def middle_kernel(got_ref, inv_ref, root_ref, out_ref, terms_ref):
    sums = jnp.sum(got_ref[:, :HALF, :].astype(f32), axis=0)
    terms = jnp.sum(got_ref[:, HALF:, :].astype(f32), axis=0)
    terms = terms[:8] + terms[8:]
    terms_ref[...] = terms
    inv, root = inv_ref[...], root_ref[...]
    vectors = inv * sums - root * (terms[0:1] / terms[1:2])
    out_ref[:, :HALF, :] = jnp.broadcast_to(
        (0.5 * inv * vectors).astype(bf16)[None], (DEPTH, HALF, LANES)
    )
    correlation = jnp.sum(root * vectors, axis=0, keepdims=True)
    hi, mid = two_parts(correlation + swap_lanes(correlation))
    index = lax.broadcasted_iota(jnp.int32, (16, LANES), 0)
    terms = jnp.where(index == 0, hi, jnp.where(index == 1, mid, 0.0)).astype(bf16)
    out_ref[:, HALF:, :] = jnp.broadcast_to(terms[None], (DEPTH, 16, LANES))


def gram_kernel(got_ref, inv_ref, root_ref, terms_ref, vectors_ref, out_ref):
    tail = got_ref[:, HALF:, :].astype(f32)
    factors = tail[:, :8].reshape(PEERS * 8, LANES).astype(bf16)
    mains = tail[:, 8:].reshape(PEERS * 8, LANES).astype(bf16)
    known = lax.dot_general(factors, mains, (((0,), (0,)), ((), ())), preferred_element_type=f32)
    sums = jnp.sum(got_ref[:, :HALF, :].astype(f32), axis=0) + known[:HALF]
    terms = jnp.sum(tail[:, 8:], axis=0)
    ratio = (terms[2:3] + terms[3:4]) / terms_ref[1:2, :]
    vectors = inv_ref[...] * sums - root_ref[...] * ratio
    vectors_ref[...] = vectors
    tall = jnp.concatenate([vectors, jnp.zeros((LANES - HALF, LANES), f32)], axis=0)
    product = jnp.dot(tall.T, tall, precision=HIGHEST, preferred_element_type=f32)
    gram = product[:K] + swap_lanes(product[K:])
    quarter = K // 2
    lane = lax.broadcasted_iota(jnp.int32, (quarter, LANES), 1)
    low = gram[quarter:]
    packed = jnp.where(lane < quarter, gram[:quarter], jnp.where(lane < K, low, swap_lanes(low)))
    tail = packed[PACKED:]
    folded = jnp.concatenate(
        [pltpu.roll(tail, LANES - quarter * (i + 1), 1) for i in range(3)], axis=0
    )
    out_ref[...] = jnp.broadcast_to(
        jnp.where(lane[:PACKED] < 3 * quarter, packed[:PACKED], folded)[None], out_ref.shape
    )


def fold_kernel(got_ref, out_ref):
    out_ref[...] = jnp.broadcast_to(jnp.sum(got_ref[...], axis=0)[None], out_ref.shape)


def solve_kernel(scale, got_ref, vectors_ref, out_ref):
    packed = jnp.sum(got_ref[...], axis=0)
    quarter = K // 2
    piece = lax.broadcasted_iota(jnp.int32, (8, LANES), 1) // quarter
    tail = jnp.zeros((8, LANES), f32)
    for i in range(3):
        tail = jnp.where(piece == i, pltpu.roll(packed[8 * i : 8 * i + 8], quarter * (i + 1), 1), tail)
    packed = jnp.concatenate([packed, tail], axis=0)
    lane = lax.broadcasted_iota(jnp.int32, packed.shape, 1)
    low = jnp.where(lane < quarter, swap_lanes(packed), packed)
    whole = jnp.concatenate([packed, low, jnp.zeros((LANES - K, LANES), f32)], axis=0)
    turned = whole.T
    upper = jnp.where(lane < quarter, packed, turned[:quarter])
    work = jnp.concatenate([upper, low], axis=0)
    row = lax.broadcasted_iota(jnp.int32, (K, LANES), 0)
    lane = lax.broadcasted_iota(jnp.int32, (K, LANES), 1)
    work = jnp.where(lane < K, work, jnp.where(lane - K == row, 1.0, 0.0))
    tiles = [work[8 * t : 8 * t + 8] for t in range(K // 8)]
    index = lax.broadcasted_iota(jnp.int32, (8, LANES), 0)
    for k in range(0, K, PIVOTS):
        first, place = divmod(k, 8)
        rows = [tiles[first][place + i : place + i + 1] for i in range(PIVOTS)]
        inner = {
            (i, j): jnp.broadcast_to(rows[i][:, k + j : k + j + 1], (1, LANES))
            for i in range(PIVOTS)
            for j in range(i, PIVOTS)
        }
        after = range(first, K // 8)
        columns = [
            {t: jnp.broadcast_to(tiles[t][:, k + i : k + i + 1], (8, LANES)) for t in after}
            for i in range(PIVOTS)
        ]
        for i in range(PIVOTS):
            inverse = 1.0 / inner[i, i]
            for m in range(i + 1, PIVOTS):
                factor = inner[i, m] * inverse
                rows[m] = rows[m] - factor * rows[i]
                for j in range(m, PIVOTS):
                    inner[m, j] = inner[m, j] - factor * inner[i, j]
                for t in after:
                    columns[m][t] = columns[m][t] - columns[i][t] * factor
            pivot_row = rows[i] * inverse
            for t in after:
                column = columns[i][t]
                if t == first:
                    column = jnp.where(index > place + i, column, 0.0)
                tiles[t] = tiles[t] - column * pivot_row
    work = jnp.concatenate(tiles, axis=0)
    pivots = jnp.sum(jnp.where(lane == row, work, 0.0), axis=1, keepdims=True)
    inv, _ = root_of(pivots)
    right = jnp.where(lane < K, 0.0, work * (inv * scale))
    low = vectors_ref[...]
    padding = jnp.zeros((2 * LANES - DOCS, LANES), f32)
    vectors = jnp.concatenate([swap_lanes(low), low, padding], axis=0)
    out_ref[...] = lax.dot_general(
        right, vectors, (((1,), (1,)), ((), ())), precision=HIGHEST, preferred_element_type=f32
    )[:, :DOCS]


def exchange(value, axes):
    return lax.all_to_all(value, axes, 0, 0, tiled=True)


def swap_core(value):
    return lax.ppermute(value, "core", [(0, 1), (1, 0)])


def shift(value, step):
    return lax.ppermute(value, "z", [(i, (i + step) % DEPTH) for i in range(DEPTH)])


def local(embeddings, start_vectors):
    all_docs = embeddings.shape[0] * lax.axis_size(AXES)
    width = E + 2 * K
    (line,) = call(
        unit_kernel,
        [shape(DOCS, width, dtype=bf16)],
        [
            pltpu.with_memory_space_constraint(value, pltpu.HBM)
            for value in (embeddings, start_vectors.T)
        ],
        [
            pltpu.VMEM((DOCS, E), bf16),
            pltpu.VMEM((K, DOCS), f32),
            pltpu.SemaphoreType.DMA((2,)),
        ],
        space=pltpu.HBM,
    )
    (plane,) = call(plane_kernel, [shape(PEERS, DOCS, E, dtype=bf16)], [line])
    pieces = [line] + [None] * (DEPTH - 1)
    behind = ahead = line
    for i in range(1, DEPTH // 2):
        behind, ahead = shift(behind, 1), shift(ahead, -1)
        pieces[-i], pieces[i] = behind, ahead
    pieces[DEPTH // 2] = shift(ahead, -1)
    (columns,) = call(
        merge_kernel, [shape(COLUMNS, width, dtype=bf16)], pieces, (), MERGE_COST
    )
    own_rows, columns = lax.optimization_barrier((exchange(plane, PLANE), columns))
    own_rows = own_rows.reshape(ROWS, E)
    other_rows = swap_core(own_rows)

    tile = shape(ROWS, COLUMNS, dtype=bf16)
    acc = pltpu.VMEM((8, COLUMNS), f32)
    flops = 2 * ROWS * COLUMNS * E
    own_tile, sums = call(
        functools.partial(tile_kernel, False),
        [tile, shape(8, COLUMNS)],
        [own_rows, columns],
        [acc],
        flops,
    )
    other_tile, sums = call(
        functools.partial(tile_kernel, True),
        [tile, shape(DEPTH, 16, LANES)],
        [other_rows, columns, sums],
        [acc],
        flops,
    )
    sums = exchange(sums, LINE)

    flops = 2 * ROWS * COLUMNS * LANES
    sent = shape(PEERS, HALF + 8, LANES)
    weights = shape(COLUMNS, LANES, dtype=bf16)
    own = shape(HALF, LANES)
    spread = pltpu.VMEM((COLUMNS, LANES), f32)
    mine, packed, inv, root = call(
        first_kernel,
        [sent, weights, own, own],
        [other_tile, sums, columns],
        [spread, spread],
        flops,
    )
    theirs = swap_core(mine)
    (mine,) = call(again_kernel, [sent], [own_tile, packed, mine], (), flops)
    halved = shape(PEERS, HALF + 16, LANES, dtype=bf16)
    (total,) = call(narrow_kernel, [halved], [mine, theirs])
    got = exchange(total, PLANE)
    total, terms = call(
        middle_kernel,
        [shape(DEPTH, HALF + 16, LANES, dtype=bf16), shape(8, LANES)],
        [got, inv, root],
    )
    got = exchange(total, LINE)
    mine, packed = call(second_kernel, [sent, weights], [other_tile, got], (), flops)
    theirs = swap_core(mine)
    (mine,) = call(again_kernel, [sent], [own_tile, packed, mine], (), flops)
    (total,) = call(split_kernel, [halved], [mine, theirs])
    got = exchange(total, PLANE)
    gram = shape(PEERS, PACKED, LANES)
    vectors, total = call(gram_kernel, [own, gram], [got, inv, root, terms])
    (total,) = call(fold_kernel, [gram], [exchange(total, (*LINE, "core"))])
    got = exchange(total, PLANE)
    (spectral,) = call(
        functools.partial(solve_kernel, math.sqrt(all_docs)), [shape(K, DOCS)], [got, vectors]
    )
    return spectral.T


def solution(mesh):
    fine = Mesh(mesh.devices.reshape(*SIZES.values()), AXES)
    return jax.shard_map(
        local,
        mesh=fine,
        in_specs=(P(AXES, None), P(AXES, None)),
        out_specs=P(AXES, None),
        check_vma=False,
    )
```

```python
import functools
import math

import jax
import jax.numpy as jnp
from jax import lax
from jax.experimental import pallas as pl
from jax.experimental.pallas import tpu as pltpu
from jax.sharding import Mesh
from jax.sharding import PartitionSpec as P

sharpness = 16.0
threshold = 0.3

AXES = ("z", "x", "y", "core")
PLANE = ("x", "y")
LINE = ("z",)
SIZES = {"z": 8, "x": 4, "y": 4, "core": 2}
DEPTH = SIZES["z"]
PEERS = SIZES["x"] * SIZES["y"]

DOCS = 192
HALF = DOCS // 2
E = 256
K = 64
COLUMNS = DEPTH * DOCS
ROWS = PEERS * DOCS
ROW_BLOCK = 3072
COLUMN_BLOCK = 768
LANES = 128
PIVOTS = 8
SAMPLE = 8
PACKED = 24
MERGE_COST = 10_350_000_000

bf16 = jnp.bfloat16
f32 = jnp.float32
HIGHEST = lax.Precision.HIGHEST


def shape(*dims, dtype=f32):
    return jax.ShapeDtypeStruct(dims, dtype)


def call(kernel, outs, args, scratch=(), flops=0, space=pltpu.VMEM, spaces=None):
    spaces = spaces or [pltpu.VMEM] * len(outs)
    moved = sum(math.prod(a.shape) * a.dtype.itemsize for a in (*args, *outs))
    return pl.pallas_call(
        kernel,
        out_shape=tuple(outs),
        in_specs=[pl.BlockSpec(memory_space=space)] * len(args),
        out_specs=tuple(pl.BlockSpec(memory_space=out) for out in spaces),
        scratch_shapes=list(scratch),
        cost_estimate=pl.CostEstimate(flops=flops, bytes_accessed=moved, transcendentals=0),
        compiler_params=pltpu.CompilerParams(vmem_limit_bytes=8 * 2**20),
    )(*args)


def left_lanes(value):
    return lax.broadcasted_iota(jnp.int32, value.shape, value.ndim - 1) < K


def swap_lanes(value):
    return pltpu.roll(value, K, value.ndim - 1)


def root_of(value):
    guess = lax.rsqrt(value)
    inv = guess * (1.5 - 0.5 * value * guess * guess)
    return inv, value * inv


def two_parts(value):
    hi = value.astype(bf16).astype(f32)
    return hi, (value - hi).astype(bf16).astype(f32)


def unit_kernel(emb_hbm, start_hbm, line_ref, plane_hbm, emb_ref, start_ref, row_ref, done, sent):
    copies = [
        pltpu.make_async_copy(emb_hbm, emb_ref, done.at[0]),
        pltpu.make_async_copy(start_hbm, start_ref, done.at[1]),
    ]
    for copy in copies:
        copy.start()
    copies[0].wait()
    wide = emb_ref[...].astype(f32)
    unit = wide * lax.rsqrt(jnp.sum(wide * wide, axis=1, keepdims=True) + 1e-06)
    unit = unit.astype(bf16)
    line_ref[:, :E] = unit
    row_ref[...] = unit * (sharpness / 2)
    outs = [pltpu.make_async_copy(row_ref, plane_hbm.at[p], sent.at[p]) for p in range(PEERS)]
    for copy in outs:
        copy.start()
    copies[1].wait()
    start = jnp.concatenate([start_ref[...], jnp.zeros((K, 2 * LANES - DOCS), f32)], axis=1)
    start = jnp.concatenate([start, jnp.zeros_like(start)], axis=0).T[:DOCS]
    hi, mid = two_parts(start)
    line_ref[:, E:] = jnp.where(left_lanes(hi), hi, swap_lanes(mid)).astype(bf16)
    for copy in outs:
        copy.wait()


def merge_kernel(*refs):
    *pieces, cols_ref = refs
    for i, piece in enumerate(pieces):
        first = (lax.axis_index("z") + i) % DEPTH * DOCS
        cols_ref[pl.ds(pl.multiple_of(first, DOCS), DOCS), :] = piece[...]


def tile_kernel(last, *refs):
    if last:
        rows_ref, cols_ref, before_ref, tile_ref, sums_ref, acc = refs
        acc[...] = before_ref[...]
    else:
        rows_ref, cols_ref, tile_ref, sums_ref, acc = refs
        acc[...] = jnp.zeros_like(acc)

    def block(i, _):
        at = pl.ds(pl.multiple_of(i * ROW_BLOCK, ROW_BLOCK), ROW_BLOCK)
        rows = rows_ref[at, :]
        for c in range(COLUMNS // COLUMN_BLOCK):
            where = slice(c * COLUMN_BLOCK, (c + 1) * COLUMN_BLOCK)
            scores = lax.dot_general(
                rows, cols_ref[where, :E], (((1,), (1,)), ((), ())), preferred_element_type=f32
            )
            entry = jnp.tanh(scores - sharpness * threshold / 2) + 1.0
            tile_ref[at, where] = entry.astype(bf16)
            acc[:, where] += jnp.sum(entry.reshape(ROW_BLOCK // 8, 8, COLUMN_BLOCK), axis=0)
        return 0

    lax.fori_loop(0, ROWS // ROW_BLOCK, block, 0)
    if last:
        total = 0.5 * jnp.sum(acc[...], axis=0, keepdims=True)
        sums_ref[...] = jnp.zeros_like(sums_ref)
        for k in range(COLUMNS // LANES):
            sums_ref[:, k : k + 1, :] = jnp.broadcast_to(
                total[None, :, k * LANES : (k + 1) * LANES], (DEPTH, 1, LANES)
            )
    else:
        sums_ref[...] = acc[...]


def multiply(tile_ref, weights_ref, out_ref, terms):
    chunks = 16

    def block(i, _):
        rows = chunks * DOCS
        sums = jnp.dot(
            tile_ref[pl.ds(pl.multiple_of(i * rows, rows), rows), :],
            weights_ref[...],
            preferred_element_type=f32,
        )
        for c in range(chunks):
            top = sums[c * DOCS : c * DOCS + HALF]
            low = sums[c * DOCS + HALF : (c + 1) * DOCS]
            out_ref[i * chunks + c, :HALF, :] = jnp.where(left_lanes(top), top, low)
            out_ref[i * chunks + c, HALF:, :] = terms
        return 0

    lax.fori_loop(0, PEERS // chunks, block, 0)


def rows_of(*values):
    index = lax.broadcasted_iota(jnp.int32, (8, LANES), 0)
    block = jnp.zeros((8, LANES), f32)
    for i, value in enumerate(values):
        block = jnp.where(index == i, jnp.broadcast_to(value, (8, LANES)), block)
    return block


def spread_lanes(packed):
    other = swap_lanes(packed)
    left = left_lanes(packed)
    return jnp.where(left, packed, other), jnp.where(left, other, packed)


def first_kernel(
    tile_ref, sums_ref, cols_ref, out_ref, weights_ref, inv_ref, root_ref, all_inv, all_root
):
    degree = jnp.sum(sums_ref[...], axis=0)
    blocks = COLUMNS // LANES
    degree = jnp.where(lax.broadcasted_iota(jnp.int32, degree.shape, 0) < blocks, degree, 1.0)
    tall = jnp.concatenate([degree, jnp.ones((LANES - degree.shape[0], LANES), f32)], axis=0).T
    inv, root = root_of(tall)
    correlation = jnp.zeros((1, LANES), f32)
    total = jnp.zeros((1, LANES), f32)
    for k in range(blocks):
        at = slice(k * LANES, (k + 1) * LANES)
        pair = cols_ref[at, E:].astype(f32)
        start = pair + swap_lanes(pair)
        own_inv = jnp.broadcast_to(inv[:, k : k + 1], (LANES, LANES))
        own_root = jnp.broadcast_to(root[:, k : k + 1], (LANES, LANES))
        all_inv[at, :] = own_inv
        all_root[at, :] = own_root
        weights_ref[at, :] = (0.5 * own_inv * start).astype(bf16)
        correlation += jnp.sum(own_root * start, axis=0, keepdims=True)
        total += jnp.sum(
            jnp.broadcast_to(tall[:, k : k + 1], (LANES, LANES)), axis=0, keepdims=True
        )
    first = lax.axis_index("z") * DOCS
    top = pl.ds(pl.multiple_of(first, HALF), HALF)
    low = pl.ds(pl.multiple_of(first + HALF, HALF), HALF)
    for whole, own in ((all_inv, inv_ref), (all_root, root_ref)):
        upper = whole[top, :]
        own[...] = jnp.where(left_lanes(upper), upper, whole[low, :])
    multiply(tile_ref, weights_ref, out_ref, rows_of(correlation, total))


def second_kernel(tile_ref, got_ref, out_ref, weights_ref):
    terms = jnp.zeros((1, LANES), f32)
    for j in range(DEPTH):
        for h, weights in enumerate(spread_lanes(got_ref[j, :HALF, :].astype(f32))):
            at = slice(j * DOCS + h * HALF, j * DOCS + (h + 1) * HALF)
            weights_ref[at, :] = weights.astype(bf16)
        terms += jnp.sum(got_ref[j, HALF:, :].astype(f32), axis=0, keepdims=True)
    multiply(tile_ref, weights_ref, out_ref, rows_of(terms))


def again_kernel(tile_ref, weights_ref, other_ref, out_ref):
    multiply(tile_ref, weights_ref, out_ref, other_ref[0, HALF:, :])


def narrow_kernel(own_ref, other_ref, out_ref):
    out_ref[:, :HALF, :] = (own_ref[:, :HALF, :] + other_ref[:, :HALF, :]).astype(bf16)
    hi, mid = two_parts(own_ref[0, HALF:, :] + other_ref[0, HALF:, :])
    terms = jnp.concatenate([hi, mid], axis=0).astype(bf16)
    out_ref[:, HALF:, :] = jnp.broadcast_to(terms[None], (PEERS, 16, LANES))


def split_kernel(own_ref, other_ref, out_ref):
    sums = own_ref[:, :HALF, :] + other_ref[:, :HALF, :]
    sample = sums[:, :SAMPLE].reshape(PEERS * SAMPLE, LANES)
    gram = lax.dot_general(sample, sample, (((0,), (0,)), ((), ())), preferred_element_type=f32)
    gram = gram[:K] + swap_lanes(gram[K:])
    gram = jnp.concatenate([jnp.where(left_lanes(gram), gram, 0.0), jnp.zeros_like(gram)], axis=0)
    main = jnp.dot(gram[:8], gram, preferred_element_type=f32)[:1]
    main = main * lax.rsqrt(jnp.sum(main * main) + 1e-30)
    main = main.astype(bf16).astype(f32)
    both = main + swap_lanes(main)
    row = lax.broadcasted_iota(jnp.int32, (LANES, LANES), 0)
    turned = jnp.where((row < K) == left_lanes(row), both, 0.0).astype(bf16)
    wide = jnp.concatenate([sums, jnp.zeros((PEERS, LANES - HALF, LANES), f32)], axis=1)
    wide = wide.reshape(PEERS * LANES, LANES).astype(bf16)
    factor = lax.dot_general(
        wide, turned, (((1,), (1,)), ((), ())), preferred_element_type=f32
    ).astype(bf16)
    known = (factor.astype(f32) * both).reshape(PEERS, LANES, LANES)
    out_ref[:, :HALF, :] = (sums - known[:, :HALF]).astype(bf16)
    index = lax.broadcasted_iota(jnp.int32, (8, LANES), 0)
    lane = lax.broadcasted_iota(jnp.int32, (8, LANES), 1)
    pick = jnp.where((lane == index * K) & (index < 2), 1.0, 0.0).astype(bf16)
    rows = lax.dot_general(pick, factor, (((1,), (1,)), ((), ())), preferred_element_type=f32)
    hi, mid = two_parts(own_ref[0, HALF : HALF + 1, :] + other_ref[0, HALF : HALF + 1, :])
    low = jnp.where(index == 0, main, jnp.where(index == 1, swap_lanes(main), 0.0))
    low = jnp.where(index == 2, hi, jnp.where(index == 3, mid, low))
    for p in range(PEERS):
        top = rows[:, p * LANES : (p + 1) * LANES]
        out_ref[p, HALF:, :] = jnp.concatenate([top, low], axis=0).astype(bf16)


def middle_kernel(got_ref, inv_ref, root_ref, out_ref, terms_ref):
    sums = jnp.sum(got_ref[:, :HALF, :].astype(f32), axis=0)
    terms = jnp.sum(got_ref[:, HALF:, :].astype(f32), axis=0)
    terms = terms[:8] + terms[8:]
    terms_ref[...] = terms
    inv, root = inv_ref[...], root_ref[...]
    vectors = inv * sums - root * (terms[0:1] / terms[1:2])
    out_ref[:, :HALF, :] = jnp.broadcast_to(
        (0.5 * inv * vectors).astype(bf16)[None], (DEPTH, HALF, LANES)
    )
    correlation = jnp.sum(root * vectors, axis=0, keepdims=True)
    hi, mid = two_parts(correlation + swap_lanes(correlation))
    index = lax.broadcasted_iota(jnp.int32, (16, LANES), 0)
    terms = jnp.where(index == 0, hi, jnp.where(index == 1, mid, 0.0)).astype(bf16)
    out_ref[:, HALF:, :] = jnp.broadcast_to(terms[None], (DEPTH, 16, LANES))


def gram_kernel(got_ref, inv_ref, root_ref, terms_ref, vectors_ref, out_ref):
    tail = got_ref[:, HALF:, :].astype(f32)
    factors = tail[:, :8].reshape(PEERS * 8, LANES).astype(bf16)
    mains = tail[:, 8:].reshape(PEERS * 8, LANES).astype(bf16)
    known = lax.dot_general(factors, mains, (((0,), (0,)), ((), ())), preferred_element_type=f32)
    sums = jnp.sum(got_ref[:, :HALF, :].astype(f32), axis=0) + known[:HALF]
    terms = jnp.sum(tail[:, 8:], axis=0)
    ratio = (terms[2:3] + terms[3:4]) / terms_ref[1:2, :]
    vectors = inv_ref[...] * sums - root_ref[...] * ratio
    vectors_ref[...] = vectors
    tall = jnp.concatenate([vectors, jnp.zeros((LANES - HALF, LANES), f32)], axis=0)
    product = jnp.dot(tall.T, tall, precision=HIGHEST, preferred_element_type=f32)
    gram = product[:K] + swap_lanes(product[K:])
    quarter = K // 2
    lane = lax.broadcasted_iota(jnp.int32, (quarter, LANES), 1)
    low = gram[quarter:]
    packed = jnp.where(lane < quarter, gram[:quarter], jnp.where(lane < K, low, swap_lanes(low)))
    tail = packed[PACKED:]
    folded = jnp.concatenate(
        [pltpu.roll(tail, LANES - quarter * (i + 1), 1) for i in range(3)], axis=0
    )
    out_ref[...] = jnp.broadcast_to(
        jnp.where(lane[:PACKED] < 3 * quarter, packed[:PACKED], folded)[None], out_ref.shape
    )


def fold_kernel(got_ref, out_ref):
    out_ref[...] = jnp.broadcast_to(jnp.sum(got_ref[...], axis=0)[None], out_ref.shape)


def solve_kernel(scale, got_ref, vectors_ref, out_ref):
    packed = jnp.sum(got_ref[...], axis=0)
    quarter = K // 2
    piece = lax.broadcasted_iota(jnp.int32, (8, LANES), 1) // quarter
    tail = jnp.zeros((8, LANES), f32)
    for i in range(3):
        tail = jnp.where(piece == i, pltpu.roll(packed[8 * i : 8 * i + 8], quarter * (i + 1), 1), tail)
    packed = jnp.concatenate([packed, tail], axis=0)
    lane = lax.broadcasted_iota(jnp.int32, packed.shape, 1)
    low = jnp.where(lane < quarter, swap_lanes(packed), packed)
    whole = jnp.concatenate([packed, low, jnp.zeros((LANES - K, LANES), f32)], axis=0)
    turned = whole.T
    upper = jnp.where(lane < quarter, packed, turned[:quarter])
    work = jnp.concatenate([upper, low], axis=0)
    row = lax.broadcasted_iota(jnp.int32, (K, LANES), 0)
    lane = lax.broadcasted_iota(jnp.int32, (K, LANES), 1)
    work = jnp.where(lane < K, work, jnp.where(lane - K == row, 1.0, 0.0))
    tiles = [work[8 * t : 8 * t + 8] for t in range(K // 8)]
    index = lax.broadcasted_iota(jnp.int32, (8, LANES), 0)
    for k in range(0, K, PIVOTS):
        first, place = divmod(k, 8)
        rows = [tiles[first][place + i : place + i + 1] for i in range(PIVOTS)]
        inner = {
            (i, j): jnp.broadcast_to(rows[i][:, k + j : k + j + 1], (1, LANES))
            for i in range(PIVOTS)
            for j in range(i, PIVOTS)
        }
        after = range(first, K // 8)
        columns = [
            {t: jnp.broadcast_to(tiles[t][:, k + i : k + i + 1], (8, LANES)) for t in after}
            for i in range(PIVOTS)
        ]
        for i in range(PIVOTS):
            inverse = 1.0 / inner[i, i]
            for m in range(i + 1, PIVOTS):
                factor = inner[i, m] * inverse
                rows[m] = rows[m] - factor * rows[i]
                for j in range(m, PIVOTS):
                    inner[m, j] = inner[m, j] - factor * inner[i, j]
                for t in after:
                    columns[m][t] = columns[m][t] - columns[i][t] * factor
            pivot_row = rows[i] * inverse
            for t in after:
                column = columns[i][t]
                if t == first:
                    column = jnp.where(index > place + i, column, 0.0)
                tiles[t] = tiles[t] - column * pivot_row
    work = jnp.concatenate(tiles, axis=0)
    pivots = jnp.sum(jnp.where(lane == row, work, 0.0), axis=1, keepdims=True)
    inv, _ = root_of(pivots)
    right = jnp.where(lane < K, 0.0, work * (inv * scale))
    low = vectors_ref[...]
    padding = jnp.zeros((2 * LANES - DOCS, LANES), f32)
    vectors = jnp.concatenate([swap_lanes(low), low, padding], axis=0)
    out_ref[...] = lax.dot_general(
        right, vectors, (((1,), (1,)), ((), ())), precision=HIGHEST, preferred_element_type=f32
    )[:, :DOCS]


def exchange(value, axes):
    return lax.all_to_all(value, axes, 0, 0, tiled=True)


def swap_core(value):
    return lax.ppermute(value, "core", [(0, 1), (1, 0)])


def shift(value, step):
    return lax.ppermute(value, "z", [(i, (i + step) % DEPTH) for i in range(DEPTH)])


def local(embeddings, start_vectors):
    all_docs = embeddings.shape[0] * lax.axis_size(AXES)
    width = E + 2 * K
    line, plane = call(
        unit_kernel,
        [shape(DOCS, width, dtype=bf16), shape(PEERS, DOCS, E, dtype=bf16)],
        [
            pltpu.with_memory_space_constraint(value, pltpu.HBM)
            for value in (embeddings, start_vectors.T)
        ],
        [
            pltpu.VMEM((DOCS, E), bf16),
            pltpu.VMEM((K, DOCS), f32),
            pltpu.VMEM((DOCS, E), bf16),
            pltpu.SemaphoreType.DMA((2,)),
            pltpu.SemaphoreType.DMA((PEERS,)),
        ],
        space=pltpu.HBM,
        spaces=[pltpu.VMEM, pltpu.HBM],
    )
    pieces = [line] + [None] * (DEPTH - 1)
    behind = ahead = line
    for i in range(1, DEPTH // 2):
        behind, ahead = shift(behind, 1), shift(ahead, -1)
        pieces[-i], pieces[i] = behind, ahead
    pieces[DEPTH // 2] = shift(ahead, -1)
    (columns,) = call(
        merge_kernel, [shape(COLUMNS, width, dtype=bf16)], pieces, (), MERGE_COST
    )
    own_rows, columns = lax.optimization_barrier((exchange(plane, PLANE), columns))
    own_rows = own_rows.reshape(ROWS, E)
    other_rows = swap_core(own_rows)

    tile = shape(ROWS, COLUMNS, dtype=bf16)
    acc = pltpu.VMEM((8, COLUMNS), f32)
    flops = 2 * ROWS * COLUMNS * E
    own_tile, sums = call(
        functools.partial(tile_kernel, False),
        [tile, shape(8, COLUMNS)],
        [own_rows, columns],
        [acc],
        flops,
    )
    other_tile, sums = call(
        functools.partial(tile_kernel, True),
        [tile, shape(DEPTH, 16, LANES)],
        [other_rows, columns, sums],
        [acc],
        flops,
    )
    sums = exchange(sums, LINE)

    flops = 2 * ROWS * COLUMNS * LANES
    sent = shape(PEERS, HALF + 8, LANES)
    weights = shape(COLUMNS, LANES, dtype=bf16)
    own = shape(HALF, LANES)
    spread = pltpu.VMEM((COLUMNS, LANES), f32)
    mine, packed, inv, root = call(
        first_kernel,
        [sent, weights, own, own],
        [other_tile, sums, columns],
        [spread, spread],
        flops,
    )
    theirs = swap_core(mine)
    (mine,) = call(again_kernel, [sent], [own_tile, packed, mine], (), flops)
    halved = shape(PEERS, HALF + 16, LANES, dtype=bf16)
    (total,) = call(narrow_kernel, [halved], [mine, theirs])
    got = exchange(total, PLANE)
    total, terms = call(
        middle_kernel,
        [shape(DEPTH, HALF + 16, LANES, dtype=bf16), shape(8, LANES)],
        [got, inv, root],
    )
    got = exchange(total, LINE)
    mine, packed = call(second_kernel, [sent, weights], [other_tile, got], (), flops)
    theirs = swap_core(mine)
    (mine,) = call(again_kernel, [sent], [own_tile, packed, mine], (), flops)
    (total,) = call(split_kernel, [halved], [mine, theirs])
    got = exchange(total, PLANE)
    gram = shape(PEERS, PACKED, LANES)
    vectors, total = call(gram_kernel, [own, gram], [got, inv, root, terms])
    (total,) = call(fold_kernel, [gram], [exchange(total, (*LINE, "core"))])
    got = exchange(total, PLANE)
    (spectral,) = call(
        functools.partial(solve_kernel, math.sqrt(all_docs)), [shape(K, DOCS)], [got, vectors]
    )
    return spectral.T


def solution(mesh):
    fine = Mesh(mesh.devices.reshape(*SIZES.values()), AXES)
    return jax.shard_map(
        local,
        mesh=fine,
        in_specs=(P(AXES, None), P(AXES, None)),
        out_specs=P(AXES, None),
        check_vma=False,
    )
```

```python
import functools
import math

import jax
import jax.numpy as jnp
from jax import lax
from jax.experimental import pallas as pl
from jax.experimental.pallas import tpu as pltpu
from jax.sharding import Mesh
from jax.sharding import PartitionSpec as P

sharpness = 16.0
threshold = 0.3

AXES = ("z", "x", "y", "core")
PLANE = ("x", "y")
LINE = ("z",)
SIZES = {"z": 8, "x": 4, "y": 4, "core": 2}
DEPTH = SIZES["z"]
PEERS = SIZES["x"] * SIZES["y"]

DOCS = 192
HALF = DOCS // 2
E = 256
K = 64
COLUMNS = DEPTH * DOCS
ROWS = PEERS * DOCS
ROW_BLOCK = 768
COLUMN_BLOCK = 256
LANES = 128
PIVOTS = 8
SAMPLE = 8
PACKED = 24
MERGE_COST = 10_350_000_000

bf16 = jnp.bfloat16
f32 = jnp.float32
HIGHEST = lax.Precision.HIGHEST


def shape(*dims, dtype=f32):
    return jax.ShapeDtypeStruct(dims, dtype)


def call(kernel, outs, args, scratch=(), flops=0, space=pltpu.VMEM, spaces=None):
    spaces = spaces or [pltpu.VMEM] * len(outs)
    moved = sum(math.prod(a.shape) * a.dtype.itemsize for a in (*args, *outs))
    return pl.pallas_call(
        kernel,
        out_shape=tuple(outs),
        in_specs=[pl.BlockSpec(memory_space=space)] * len(args),
        out_specs=tuple(pl.BlockSpec(memory_space=out) for out in spaces),
        scratch_shapes=list(scratch),
        cost_estimate=pl.CostEstimate(flops=flops, bytes_accessed=moved, transcendentals=0),
        compiler_params=pltpu.CompilerParams(vmem_limit_bytes=8 * 2**20),
    )(*args)


def left_lanes(value):
    return lax.broadcasted_iota(jnp.int32, value.shape, value.ndim - 1) < K


def swap_lanes(value):
    return pltpu.roll(value, K, value.ndim - 1)


def root_of(value):
    guess = lax.rsqrt(value)
    inv = guess * (1.5 - 0.5 * value * guess * guess)
    return inv, value * inv


def two_parts(value):
    hi = value.astype(bf16).astype(f32)
    return hi, (value - hi).astype(bf16).astype(f32)


def unit_kernel(emb_hbm, start_hbm, line_ref, plane_hbm, emb_ref, start_ref, row_ref, done, sent):
    copies = [
        pltpu.make_async_copy(emb_hbm, emb_ref, done.at[0]),
        pltpu.make_async_copy(start_hbm, start_ref, done.at[1]),
    ]
    for copy in copies:
        copy.start()
    copies[0].wait()
    wide = emb_ref[...].astype(f32)
    unit = wide * lax.rsqrt(jnp.sum(wide * wide, axis=1, keepdims=True) + 1e-06)
    unit = unit.astype(bf16)
    line_ref[:, :E] = unit
    row_ref[...] = unit * (sharpness / 2)
    outs = [pltpu.make_async_copy(row_ref, plane_hbm.at[p], sent.at[p]) for p in range(PEERS)]
    for copy in outs:
        copy.start()
    copies[1].wait()
    start = jnp.concatenate([start_ref[...], jnp.zeros((K, 2 * LANES - DOCS), f32)], axis=1)
    start = jnp.concatenate([start, jnp.zeros_like(start)], axis=0).T[:DOCS]
    hi, mid = two_parts(start)
    line_ref[:, E:] = jnp.where(left_lanes(hi), hi, swap_lanes(mid)).astype(bf16)
    for copy in outs:
        copy.wait()


def merge_kernel(*refs):
    *pieces, cols_ref = refs
    for i, piece in enumerate(pieces):
        first = (lax.axis_index("z") + i) % DEPTH * DOCS
        cols_ref[pl.ds(pl.multiple_of(first, DOCS), DOCS), :] = piece[...]


def tile_kernel(last, *refs):
    if last:
        rows_ref, cols_ref, before_ref, tile_ref, sums_ref, acc = refs
        acc[...] = before_ref[...]
    else:
        rows_ref, cols_ref, tile_ref, sums_ref, acc = refs
        acc[...] = jnp.zeros_like(acc)

    for c in range(COLUMNS // COLUMN_BLOCK):
        where = slice(c * COLUMN_BLOCK, (c + 1) * COLUMN_BLOCK)
        sums = jnp.zeros((8, COLUMN_BLOCK), f32)
        for r in range(ROWS // ROW_BLOCK):
            at = slice(r * ROW_BLOCK, (r + 1) * ROW_BLOCK)
            scores = lax.dot_general(
                rows_ref[at, :],
                cols_ref[where, :E],
                (((1,), (1,)), ((), ())),
                preferred_element_type=f32,
            )
            entry = jnp.tanh(scores - sharpness * threshold / 2) + 1.0
            tile_ref[at, where] = entry.astype(bf16)
            sums += jnp.sum(entry.reshape(ROW_BLOCK // 8, 8, COLUMN_BLOCK), axis=0)
        acc[:, where] += sums

    if last:
        total = 0.5 * jnp.sum(acc[...], axis=0, keepdims=True)
        sums_ref[...] = jnp.zeros_like(sums_ref)
        for k in range(COLUMNS // LANES):
            sums_ref[:, k : k + 1, :] = jnp.broadcast_to(
                total[None, :, k * LANES : (k + 1) * LANES], (DEPTH, 1, LANES)
            )
    else:
        sums_ref[...] = acc[...]


def multiply(tile_ref, weights_ref, out_ref, terms):
    chunks = 16

    def block(i, _):
        rows = chunks * DOCS
        sums = jnp.dot(
            tile_ref[pl.ds(pl.multiple_of(i * rows, rows), rows), :],
            weights_ref[...],
            preferred_element_type=f32,
        )
        for c in range(chunks):
            top = sums[c * DOCS : c * DOCS + HALF]
            low = sums[c * DOCS + HALF : (c + 1) * DOCS]
            out_ref[i * chunks + c, :HALF, :] = jnp.where(left_lanes(top), top, low)
            out_ref[i * chunks + c, HALF:, :] = terms
        return 0

    lax.fori_loop(0, PEERS // chunks, block, 0)


def rows_of(*values):
    index = lax.broadcasted_iota(jnp.int32, (8, LANES), 0)
    block = jnp.zeros((8, LANES), f32)
    for i, value in enumerate(values):
        block = jnp.where(index == i, jnp.broadcast_to(value, (8, LANES)), block)
    return block


def spread_lanes(packed):
    other = swap_lanes(packed)
    left = left_lanes(packed)
    return jnp.where(left, packed, other), jnp.where(left, other, packed)


def first_kernel(
    tile_ref, sums_ref, cols_ref, out_ref, weights_ref, inv_ref, root_ref, all_inv, all_root
):
    degree = jnp.sum(sums_ref[...], axis=0)
    blocks = COLUMNS // LANES
    degree = jnp.where(lax.broadcasted_iota(jnp.int32, degree.shape, 0) < blocks, degree, 1.0)
    tall = jnp.concatenate([degree, jnp.ones((LANES - degree.shape[0], LANES), f32)], axis=0).T
    inv, root = root_of(tall)
    correlation = jnp.zeros((1, LANES), f32)
    total = jnp.zeros((1, LANES), f32)
    for k in range(blocks):
        at = slice(k * LANES, (k + 1) * LANES)
        pair = cols_ref[at, E:].astype(f32)
        start = pair + swap_lanes(pair)
        own_inv = jnp.broadcast_to(inv[:, k : k + 1], (LANES, LANES))
        own_root = jnp.broadcast_to(root[:, k : k + 1], (LANES, LANES))
        all_inv[at, :] = own_inv
        all_root[at, :] = own_root
        weights_ref[at, :] = (0.5 * own_inv * start).astype(bf16)
        correlation += jnp.sum(own_root * start, axis=0, keepdims=True)
        total += jnp.sum(
            jnp.broadcast_to(tall[:, k : k + 1], (LANES, LANES)), axis=0, keepdims=True
        )
    first = lax.axis_index("z") * DOCS
    top = pl.ds(pl.multiple_of(first, HALF), HALF)
    low = pl.ds(pl.multiple_of(first + HALF, HALF), HALF)
    for whole, own in ((all_inv, inv_ref), (all_root, root_ref)):
        upper = whole[top, :]
        own[...] = jnp.where(left_lanes(upper), upper, whole[low, :])
    multiply(tile_ref, weights_ref, out_ref, rows_of(correlation, total))


def second_kernel(tile_ref, got_ref, out_ref, weights_ref):
    terms = jnp.zeros((1, LANES), f32)
    for j in range(DEPTH):
        for h, weights in enumerate(spread_lanes(got_ref[j, :HALF, :].astype(f32))):
            at = slice(j * DOCS + h * HALF, j * DOCS + (h + 1) * HALF)
            weights_ref[at, :] = weights.astype(bf16)
        terms += jnp.sum(got_ref[j, HALF:, :].astype(f32), axis=0, keepdims=True)
    multiply(tile_ref, weights_ref, out_ref, rows_of(terms))


def again_kernel(tile_ref, weights_ref, other_ref, out_ref):
    multiply(tile_ref, weights_ref, out_ref, other_ref[0, HALF:, :])


def narrow_kernel(own_ref, other_ref, out_ref):
    out_ref[:, :HALF, :] = (own_ref[:, :HALF, :] + other_ref[:, :HALF, :]).astype(bf16)
    hi, mid = two_parts(own_ref[0, HALF:, :] + other_ref[0, HALF:, :])
    terms = jnp.concatenate([hi, mid], axis=0).astype(bf16)
    out_ref[:, HALF:, :] = jnp.broadcast_to(terms[None], (PEERS, 16, LANES))


def split_kernel(own_ref, other_ref, out_ref):
    sums = own_ref[:, :HALF, :] + other_ref[:, :HALF, :]
    sample = sums[:, :SAMPLE].reshape(PEERS * SAMPLE, LANES)
    gram = lax.dot_general(sample, sample, (((0,), (0,)), ((), ())), preferred_element_type=f32)
    gram = gram[:K] + swap_lanes(gram[K:])
    gram = jnp.concatenate([jnp.where(left_lanes(gram), gram, 0.0), jnp.zeros_like(gram)], axis=0)
    main = jnp.dot(gram[:8], gram, preferred_element_type=f32)[:1]
    main = main * lax.rsqrt(jnp.sum(main * main) + 1e-30)
    main = main.astype(bf16).astype(f32)
    both = main + swap_lanes(main)
    row = lax.broadcasted_iota(jnp.int32, (LANES, LANES), 0)
    turned = jnp.where((row < K) == left_lanes(row), both, 0.0).astype(bf16)
    wide = jnp.concatenate([sums, jnp.zeros((PEERS, LANES - HALF, LANES), f32)], axis=1)
    wide = wide.reshape(PEERS * LANES, LANES).astype(bf16)
    factor = lax.dot_general(
        wide, turned, (((1,), (1,)), ((), ())), preferred_element_type=f32
    ).astype(bf16)
    known = (factor.astype(f32) * both).reshape(PEERS, LANES, LANES)
    out_ref[:, :HALF, :] = (sums - known[:, :HALF]).astype(bf16)
    index = lax.broadcasted_iota(jnp.int32, (8, LANES), 0)
    lane = lax.broadcasted_iota(jnp.int32, (8, LANES), 1)
    pick = jnp.where((lane == index * K) & (index < 2), 1.0, 0.0).astype(bf16)
    rows = lax.dot_general(pick, factor, (((1,), (1,)), ((), ())), preferred_element_type=f32)
    hi, mid = two_parts(own_ref[0, HALF : HALF + 1, :] + other_ref[0, HALF : HALF + 1, :])
    low = jnp.where(index == 0, main, jnp.where(index == 1, swap_lanes(main), 0.0))
    low = jnp.where(index == 2, hi, jnp.where(index == 3, mid, low))
    for p in range(PEERS):
        top = rows[:, p * LANES : (p + 1) * LANES]
        out_ref[p, HALF:, :] = jnp.concatenate([top, low], axis=0).astype(bf16)


def middle_kernel(got_ref, inv_ref, root_ref, out_ref, terms_ref):
    sums = jnp.sum(got_ref[:, :HALF, :].astype(f32), axis=0)
    terms = jnp.sum(got_ref[:, HALF:, :].astype(f32), axis=0)
    terms = terms[:8] + terms[8:]
    terms_ref[...] = terms
    inv, root = inv_ref[...], root_ref[...]
    vectors = inv * sums - root * (terms[0:1] / terms[1:2])
    out_ref[:, :HALF, :] = jnp.broadcast_to(
        (0.5 * inv * vectors).astype(bf16)[None], (DEPTH, HALF, LANES)
    )
    correlation = jnp.sum(root * vectors, axis=0, keepdims=True)
    hi, mid = two_parts(correlation + swap_lanes(correlation))
    index = lax.broadcasted_iota(jnp.int32, (16, LANES), 0)
    terms = jnp.where(index == 0, hi, jnp.where(index == 1, mid, 0.0)).astype(bf16)
    out_ref[:, HALF:, :] = jnp.broadcast_to(terms[None], (DEPTH, 16, LANES))


def gram_kernel(got_ref, inv_ref, root_ref, terms_ref, vectors_ref, out_ref):
    tail = got_ref[:, HALF:, :].astype(f32)
    factors = tail[:, :8].reshape(PEERS * 8, LANES).astype(bf16)
    mains = tail[:, 8:].reshape(PEERS * 8, LANES).astype(bf16)
    known = lax.dot_general(factors, mains, (((0,), (0,)), ((), ())), preferred_element_type=f32)
    sums = jnp.sum(got_ref[:, :HALF, :].astype(f32), axis=0) + known[:HALF]
    terms = jnp.sum(tail[:, 8:], axis=0)
    ratio = (terms[2:3] + terms[3:4]) / terms_ref[1:2, :]
    vectors = inv_ref[...] * sums - root_ref[...] * ratio
    vectors_ref[...] = vectors
    tall = jnp.concatenate([vectors, jnp.zeros((LANES - HALF, LANES), f32)], axis=0)
    product = jnp.dot(tall.T, tall, precision=HIGHEST, preferred_element_type=f32)
    gram = product[:K] + swap_lanes(product[K:])
    quarter = K // 2
    lane = lax.broadcasted_iota(jnp.int32, (quarter, LANES), 1)
    low = gram[quarter:]
    packed = jnp.where(lane < quarter, gram[:quarter], jnp.where(lane < K, low, swap_lanes(low)))
    tail = packed[PACKED:]
    folded = jnp.concatenate(
        [pltpu.roll(tail, LANES - quarter * (i + 1), 1) for i in range(3)], axis=0
    )
    out_ref[...] = jnp.broadcast_to(
        jnp.where(lane[:PACKED] < 3 * quarter, packed[:PACKED], folded)[None], out_ref.shape
    )


def fold_kernel(got_ref, out_ref):
    out_ref[...] = jnp.broadcast_to(jnp.sum(got_ref[...], axis=0)[None], out_ref.shape)


def solve_kernel(scale, got_ref, vectors_ref, out_ref):
    packed = jnp.sum(got_ref[...], axis=0)
    quarter = K // 2
    piece = lax.broadcasted_iota(jnp.int32, (8, LANES), 1) // quarter
    tail = jnp.zeros((8, LANES), f32)
    for i in range(3):
        tail = jnp.where(piece == i, pltpu.roll(packed[8 * i : 8 * i + 8], quarter * (i + 1), 1), tail)
    packed = jnp.concatenate([packed, tail], axis=0)
    lane = lax.broadcasted_iota(jnp.int32, packed.shape, 1)
    low = jnp.where(lane < quarter, swap_lanes(packed), packed)
    whole = jnp.concatenate([packed, low, jnp.zeros((LANES - K, LANES), f32)], axis=0)
    turned = whole.T
    upper = jnp.where(lane < quarter, packed, turned[:quarter])
    work = jnp.concatenate([upper, low], axis=0)
    row = lax.broadcasted_iota(jnp.int32, (K, LANES), 0)
    lane = lax.broadcasted_iota(jnp.int32, (K, LANES), 1)
    work = jnp.where(lane < K, work, jnp.where(lane - K == row, 1.0, 0.0))
    tiles = [work[8 * t : 8 * t + 8] for t in range(K // 8)]
    index = lax.broadcasted_iota(jnp.int32, (8, LANES), 0)
    for k in range(0, K, PIVOTS):
        first, place = divmod(k, 8)
        rows = [tiles[first][place + i : place + i + 1] for i in range(PIVOTS)]
        inner = {
            (i, j): jnp.broadcast_to(rows[i][:, k + j : k + j + 1], (1, LANES))
            for i in range(PIVOTS)
            for j in range(i, PIVOTS)
        }
        after = range(first, K // 8)
        columns = [
            {t: jnp.broadcast_to(tiles[t][:, k + i : k + i + 1], (8, LANES)) for t in after}
            for i in range(PIVOTS)
        ]
        for i in range(PIVOTS):
            inverse = 1.0 / inner[i, i]
            for m in range(i + 1, PIVOTS):
                factor = inner[i, m] * inverse
                rows[m] = rows[m] - factor * rows[i]
                for j in range(m, PIVOTS):
                    inner[m, j] = inner[m, j] - factor * inner[i, j]
                for t in after:
                    columns[m][t] = columns[m][t] - columns[i][t] * factor
            pivot_row = rows[i] * inverse
            for t in after:
                column = columns[i][t]
                if t == first:
                    column = jnp.where(index > place + i, column, 0.0)
                tiles[t] = tiles[t] - column * pivot_row
    work = jnp.concatenate(tiles, axis=0)
    pivots = jnp.sum(jnp.where(lane == row, work, 0.0), axis=1, keepdims=True)
    inv, _ = root_of(pivots)
    right = jnp.where(lane < K, 0.0, work * (inv * scale))
    low = vectors_ref[...]
    padding = jnp.zeros((2 * LANES - DOCS, LANES), f32)
    vectors = jnp.concatenate([swap_lanes(low), low, padding], axis=0)
    out_ref[...] = lax.dot_general(
        right, vectors, (((1,), (1,)), ((), ())), precision=HIGHEST, preferred_element_type=f32
    )[:, :DOCS]


def exchange(value, axes):
    return lax.all_to_all(value, axes, 0, 0, tiled=True)


def swap_core(value):
    return lax.ppermute(value, "core", [(0, 1), (1, 0)])


def shift(value, step):
    return lax.ppermute(value, "z", [(i, (i + step) % DEPTH) for i in range(DEPTH)])


def local(embeddings, start_vectors):
    all_docs = embeddings.shape[0] * lax.axis_size(AXES)
    width = E + 2 * K
    line, plane = call(
        unit_kernel,
        [shape(DOCS, width, dtype=bf16), shape(PEERS, DOCS, E, dtype=bf16)],
        [
            pltpu.with_memory_space_constraint(value, pltpu.HBM)
            for value in (embeddings, start_vectors.T)
        ],
        [
            pltpu.VMEM((DOCS, E), bf16),
            pltpu.VMEM((K, DOCS), f32),
            pltpu.VMEM((DOCS, E), bf16),
            pltpu.SemaphoreType.DMA((2,)),
            pltpu.SemaphoreType.DMA((PEERS,)),
        ],
        space=pltpu.HBM,
        spaces=[pltpu.VMEM, pltpu.HBM],
    )
    pieces = [line] + [None] * (DEPTH - 1)
    behind = ahead = line
    for i in range(1, DEPTH // 2):
        behind, ahead = shift(behind, 1), shift(ahead, -1)
        pieces[-i], pieces[i] = behind, ahead
    pieces[DEPTH // 2] = shift(ahead, -1)
    (columns,) = call(
        merge_kernel, [shape(COLUMNS, width, dtype=bf16)], pieces, (), MERGE_COST
    )
    own_rows, columns = lax.optimization_barrier((exchange(plane, PLANE), columns))
    own_rows = own_rows.reshape(ROWS, E)
    other_rows = swap_core(own_rows)

    tile = shape(ROWS, COLUMNS, dtype=bf16)
    acc = pltpu.VMEM((8, COLUMNS), f32)
    flops = 2 * ROWS * COLUMNS * E
    own_tile, sums = call(
        functools.partial(tile_kernel, False),
        [tile, shape(8, COLUMNS)],
        [own_rows, columns],
        [acc],
        flops,
    )
    other_tile, sums = call(
        functools.partial(tile_kernel, True),
        [tile, shape(DEPTH, 16, LANES)],
        [other_rows, columns, sums],
        [acc],
        flops,
    )
    sums = exchange(sums, LINE)

    flops = 2 * ROWS * COLUMNS * LANES
    sent = shape(PEERS, HALF + 8, LANES)
    weights = shape(COLUMNS, LANES, dtype=bf16)
    own = shape(HALF, LANES)
    spread = pltpu.VMEM((COLUMNS, LANES), f32)
    mine, packed, inv, root = call(
        first_kernel,
        [sent, weights, own, own],
        [other_tile, sums, columns],
        [spread, spread],
        flops,
    )
    theirs = swap_core(mine)
    (mine,) = call(again_kernel, [sent], [own_tile, packed, mine], (), flops)
    halved = shape(PEERS, HALF + 16, LANES, dtype=bf16)
    (total,) = call(narrow_kernel, [halved], [mine, theirs])
    got = exchange(total, PLANE)
    total, terms = call(
        middle_kernel,
        [shape(DEPTH, HALF + 16, LANES, dtype=bf16), shape(8, LANES)],
        [got, inv, root],
    )
    got = exchange(total, LINE)
    mine, packed = call(second_kernel, [sent, weights], [other_tile, got], (), flops)
    theirs = swap_core(mine)
    (mine,) = call(again_kernel, [sent], [own_tile, packed, mine], (), flops)
    (total,) = call(split_kernel, [halved], [mine, theirs])
    got = exchange(total, PLANE)
    gram = shape(PEERS, PACKED, LANES)
    vectors, total = call(gram_kernel, [own, gram], [got, inv, root, terms])
    (total,) = call(fold_kernel, [gram], [exchange(total, (*LINE, "core"))])
    got = exchange(total, PLANE)
    (spectral,) = call(
        functools.partial(solve_kernel, math.sqrt(all_docs)), [shape(K, DOCS)], [got, vectors]
    )
    return spectral.T


def solution(mesh):
    fine = Mesh(mesh.devices.reshape(*SIZES.values()), AXES)
    return jax.shard_map(
        local,
        mesh=fine,
        in_specs=(P(AXES, None), P(AXES, None)),
        out_specs=P(AXES, None),
        check_vma=False,
    )
```
